256 devices in a mesh: tm: 16 (over z, core), expert: 16 (over y, x).
Axes of the slice: x: 4, y: 4, z: 8, core: 2. Of those that a mesh axis runs over, the one named last changes fastest.
Arguments:
- tokens: bfloat16 [16, 16, 128, 2048], P('expert', 'tm'), may hold values from -29 to 29
- queries: bfloat16 [16, 16, 128, 2048], P('expert', 'tm'), may hold values from -40 to 40
- key_rows: bfloat16 [16, 16, 128, 2048], P('expert', 'tm'), may hold values from -7 to 7
- values: bfloat16 [16, 16, 128, 2048], P('expert', 'tm'), may hold values from -18 to 18
- actions: int32 [16, 16], P('expert', 'tm'), may hold values from 0 to 63
- action_table: bfloat16 [64, 2048], replicated, may hold values from -6 to 6
- norm_gain: float32 [2048], replicated, may hold values from 0.5 to 1.5
- routes: int32 [16, 16, 128, 2], P('expert', 'tm'), may hold values from 0 to 15, all different within a row; in each aligned block of 128 rows (0 to 127, 128 to 255, ..., all dimensions but the last counted through in order) at most 20 rows name the same one
- gate_probs: float32 [16, 16, 128, 2], P('expert', 'tm'), may hold values from 0.1 to 1
- predicted: int32 [16, 16, 128], P('expert', 'tm'), may hold values 0 or 1
- cotangent: bfloat16 [16, 16, 128, 2048], P('expert', 'tm'), may hold values from -0.8984375 to 0.8984375
- up_weight: bfloat16 [16, 2048, 1024], P('expert'), may hold values from -0.125 to 0.125
- down_weight: bfloat16 [16, 1024, 2048], P('expert'), may hold values from -0.1875 to 0.1875
Outputs:
- layer_out: bfloat16 [16, 16, 128, 2048], P('expert', 'tm')
- stream_grad: bfloat16 [16, 16, 128, 2048], P('expert', 'tm')
- up_grad: bfloat16 [16, 2048, 1024], P('expert', 'tm')
- down_grad: bfloat16 [16, 1024, 2048], P('expert', 'tm')
The draws below stay inside these ranges and needn't reach their ends.
Inputs may be any that keep to these rules, and one draw needn't show every extreme that they name: `routes`: in the 128 tokens of one frame of one clip the 2 experts of a token differ, no expert is named more than 20 times, a bound that some block reaches.
All inputs are finite; a program needn't handle non-finite values. No bound on the sum of `predicted` on one device may be relied on, other than what follows from the above.
Results may differ from the reference program's by a relative error of at most 0.018.
Values may be sent and summed in bfloat16 or wider, within the bound.
A program may use at most 128 MiB of HBM per device.

```python
import math
import jax
import jax.numpy as jnp
import numpy as np
from jax import lax

D = 2048
HEADS = 16
HD = 128
FF = 1024
ACTIONS = 64
TOPK = 2
FTOK = 128
FRAMES = 16
CLIPS = 16
EXPERTS = 16
CAP = 20


def query_key_pair(key):
    base = jax.random.fold_in(key, 31)
    first, second = jax.random.split(base, 2)
    full_shape = (CLIPS, FRAMES, FTOK, D)
    key_draw = jnp.clip(jax.random.normal(second, full_shape, jnp.float32), -6.0, 6.0)
    query_draw = 2.0 * jnp.clip(jax.random.normal(first, full_shape, jnp.float32), -6.0, 6.0)
    return (query_draw, key_draw)


def draw_queries(key, part):
    return query_key_pair(key)[0].astype(jnp.bfloat16)


def draw_key_rows(key, part):
    return query_key_pair(key)[1].astype(jnp.bfloat16)


def draw_tokens(key, part):
    base = jax.random.fold_in(key, 11)
    first, second = jax.random.split(base, 2)
    full_shape = (CLIPS, FRAMES, FTOK, D)
    column_scale = jnp.exp(jax.random.uniform(second, (D,), jnp.float32, -1.2, 1.2))
    return (jnp.clip(jax.random.normal(first, full_shape, jnp.float32), -6.0, 6.0) * column_scale).astype(jnp.bfloat16)


def with_ends(result, stream_key, least, top_value):
    index_at = [jax.random.randint(jax.random.fold_in(stream_key, axis), (), 0, length) for axis, length in enumerate(result.shape)]
    widest = result.shape.index(max(result.shape))
    beside = index_at[:widest] + [(index_at[widest] + 1) % result.shape[widest]] + index_at[widest + 1:]
    return result.at[tuple(index_at)].set(least).at[tuple(beside)].set(top_value)


def block_scale(key, shape, pieces, low, largest):
    def one(dim, parts):
        heights = jax.random.uniform(jax.random.fold_in(jax.random.fold_in(key, 6), dim), (parts,), jnp.float32, low / len(pieces), largest / len(pieces))
        return jnp.repeat(jnp.exp(heights), shape[dim] // parts).reshape((-1,) + (1,) * (len(shape) - dim - 1))

    loudness = one(*pieces[0])
    for cut in pieces[1:]:
        loudness = loudness * one(*cut)
    return loudness


def routed_block(key, own, number, rows, amount, top, limit, lean):
    ranking = jax.random.permutation(key, amount)
    packed, common = shares(amount, rows * top, limit, lean, True), shares(amount, rows * top, limit, lean, False)
    places = jnp.arange(amount)

    def named(sizes, turn):
        used = int((sizes > 0).sum())
        fixed = max(1, used // 4)
        shifted = fixed + (places - fixed + turn * (used - fixed)) % max(1, amount - fixed)
        return jnp.zeros((amount,), jnp.int32).at[ranking[jnp.where(places < fixed, places, shifted)]].set(jnp.asarray(sizes, jnp.int32))

    sizes = jnp.where(number % 4 == 0, named(packed, number // 4), named(common, number - number // 4 - 1))
    mixed = jax.random.permutation(jax.random.fold_in(own, 3), amount)
    donor, receiver = mixed[0:amount // 2 * 2:2], mixed[1:amount // 2 * 2:2]
    slack = jnp.minimum(sizes[donor] - 1, limit - sizes[receiver]) // 2
    slack = jnp.where((donor == ranking[0]) | (receiver == ranking[0]) | (sizes[receiver] == 0), 0, jnp.maximum(slack, 0))
    shifted = jax.random.randint(jax.random.fold_in(own, 4), (amount // 2,), 0, 1 << 20) % (slack + 1)
    sizes = sizes.at[donor].add(-shifted).at[receiver].add(shifted)
    members = jnp.searchsorted(jnp.cumsum(sizes), jnp.arange(rows * top), side="right").astype(jnp.int32)
    grid = members.reshape(top, rows).T
    grid = grid[jax.random.permutation(jax.random.fold_in(own, 1), rows)]
    turn = jax.random.randint(jax.random.fold_in(own, 2), (rows, 1), 0, top)
    return jnp.take_along_axis(grid, (jnp.arange(top)[None, :] + turn) % top, axis=1)


def shares(number_of, total, most, lean, full):
    loads = [(1 << 20) // math.isqrt(grade ** lean) + 1 for grade in range(1, number_of + 1)]
    largest = most if full else min(most, max(-(-total // number_of), total * loads[0] // sum(loads)))
    least = 1 if total - largest >= number_of - 1 else 0
    given, rest = [largest] + [least] * (number_of - 1), total - largest - least * (number_of - 1)
    while rest > 0:
        candidates = [i for i in range(1, number_of) if given[i] < largest] or [i for i in range(1, number_of) if given[i] < most]
        pool, budget = sum([loads[i] for i in candidates]), rest
        for i in candidates:
            addition = min(most - given[i], max(1, budget * loads[i] // pool), rest)
            given[i] = given[i] + addition
            rest = rest - addition
    return np.array(given)


def bell_draw(key, shape, deviation, reach, cuts=(), held_as=jnp.bfloat16):
    drawn = jax.random.normal(key, shape, jnp.float32) * deviation
    if len(cuts) > 0:
        drawn = block_scale(key, shape, cuts, -0.22, 0.18) * drawn
    return jnp.clip(drawn, min=-reach, max=reach).astype(held_as)


def setup_inputs(seed: int = 0) -> dict:
    splits = jax.random.split(jax.random.key(seed), 14)
    tokens = draw_tokens(jax.random.fold_in(splits[13], 71), 0)
    queries = draw_queries(jax.random.fold_in(splits[13], 71), 0)
    key_rows = draw_key_rows(jax.random.fold_in(splits[13], 71), 0)
    values = bell_draw(splits[3], (CLIPS, FRAMES, FTOK, D), 3.0, 18.0, ((0, 16), (1, 16)))
    actions = with_ends(jax.random.randint(splits[4], (CLIPS, FRAMES), 0, ACTIONS), jax.random.fold_in(splits[4], 1), 0, ACTIONS - 1).astype(jnp.int32)
    action_table = bell_draw(splits[5], (ACTIONS, D), 1.0, 6.0)
    norm_gain = jnp.clip(1.0 + 0.1 * jax.random.normal(splits[6], (D,), jnp.float32), 0.5, 1.5)
    routes_keys = jax.random.split(jax.random.fold_in(splits[7], 1), CLIPS * FRAMES * FTOK // FTOK)
    routes_turns = jax.random.permutation(jax.random.fold_in(splits[7], 3), CLIPS * FRAMES * FTOK // FTOK)
    routes = jax.vmap(lambda own, number: routed_block(jax.random.fold_in(splits[7], 2), own, number, FTOK, EXPERTS, TOPK, CAP, 2))(routes_keys, routes_turns).reshape((CLIPS, FRAMES, FTOK, TOPK))
    gate_probs = jnp.clip(jnp.exp(math.log(1.0) - 2.3025851 * jax.random.uniform(splits[8], (CLIPS, FRAMES, FTOK, TOPK), jnp.float32) ** block_scale(splits[8], (CLIPS, FRAMES, FTOK, TOPK), ((0, 16), (1, 16)), -0.2, 0.2)), 0.1, 1.0)
    predicted = with_ends((jax.random.randint(splits[9], (CLIPS, FRAMES, FTOK), 0, 2) < 1).astype(jnp.int32), jax.random.fold_in(splits[9], 1), 0, 1)
    cotangent = bell_draw(splits[10], (CLIPS, FRAMES, FTOK, D), 0.15, 0.8984375, ((0, 16), (1, 16)))
    up_weight = bell_draw(splits[11], (EXPERTS, D, FF), D ** -0.5, 0.125, ((0, 16),))
    down_weight = bell_draw(splits[12], (EXPERTS, FF, D), FF ** -0.5, 0.1875, ((0, 16),))
    return {"tokens": tokens, "queries": queries, "key_rows": key_rows, "values": values, "actions": actions, "action_table": action_table, "norm_gain": norm_gain, "routes": routes, "gate_probs": gate_probs, "predicted": predicted, "cotangent": cotangent, "up_weight": up_weight, "down_weight": down_weight}


norm_eps = 1e-06
gelu_coef = 0.7978845608028654

def gelu_value(preact):
    inner = gelu_coef * (preact + 0.044715 * preact * preact * preact)
    return 0.5 * preact * (1.0 + jnp.tanh(inner))

def gelu_slope(preact):
    tanh_inner = jnp.tanh(gelu_coef * (preact + 0.044715 * preact * preact * preact))
    return 0.5 * (1.0 + tanh_inner) + 0.5 * preact * (1.0 - tanh_inner * tanh_inner) * gelu_coef * (1.0 + 3.0 * 0.044715 * preact * preact)

def attend(triple):
    query_blk, key_blk, value_blk = triple
    key_span = FRAMES * FTOK
    query_f32 = query_blk.reshape(key_span, HEADS, HD).astype(jnp.float32)
    key_f32 = key_blk.reshape(key_span, HEADS, HD).astype(jnp.float32)
    value_f32 = value_blk.reshape(key_span, HEADS, HD).astype(jnp.float32)
    scores = jnp.einsum('qhd,khd->hqk', query_f32, key_f32) * HD ** (-0.5)
    frame_ids = jnp.arange(key_span, dtype=jnp.int32) // FTOK
    allowed = frame_ids[None, :] <= frame_ids[:, None]
    scores = jnp.where(allowed[None], scores, -1e+30)
    maximum = lax.optimization_barrier(jnp.max(scores, -1, keepdims=True))
    exponent = jnp.exp(scores - maximum)
    weights = (exponent / lax.optimization_barrier(jnp.sum(exponent, -1, keepdims=True))).astype(jnp.bfloat16)
    attention_out = jnp.einsum('hqk,khd->qhd', weights.astype(jnp.float32), value_f32)
    return attention_out.reshape(FRAMES, FTOK, D)

def reference(tokens, queries, key_rows, values, actions, action_table, norm_gain, routes, gate_probs, predicted, cotangent, up_weight, down_weight):
    block_count = CLIPS * FRAMES
    pair_count = FTOK * TOPK
    attended = lax.map(attend, (queries, key_rows, values))
    action_rows = action_table[actions].astype(jnp.float32)
    stream = (tokens.astype(jnp.float32) + attended + action_rows[:, :, None, :]).astype(jnp.bfloat16)
    stream = lax.optimization_barrier(stream)
    stream_f32 = stream.astype(jnp.float32)
    inv_rms = lax.rsqrt(lax.optimization_barrier(jnp.mean(stream_f32 * stream_f32, -1, keepdims=True)) + norm_eps)
    unit_rows = stream_f32 * inv_rms
    normed = (unit_rows * norm_gain).astype(jnp.bfloat16)
    flat_routes = routes.reshape(block_count, pair_count)
    expert_hits = (flat_routes[:, :, None] == jnp.arange(EXPERTS, dtype=jnp.int32)).astype(jnp.int32)
    earlier = jnp.cumsum(expert_hits, 1) - expert_hits
    slot_rank = lax.optimization_barrier(jnp.sum(earlier * expert_hits, -1))
    block_ids = jnp.arange(block_count, dtype=jnp.int32)
    clip_ids = block_ids // FRAMES
    frame_ids = block_ids % FRAMES
    position = ((flat_routes * FRAMES + frame_ids[:, None]) * CLIPS + clip_ids[:, None]) * CAP + slot_rank
    position = position.reshape(-1).astype(jnp.int32)
    rows_total = EXPERTS * FRAMES * CLIPS * CAP
    token_rows = jnp.repeat(normed.reshape(block_count * FTOK, D), TOPK, axis=0)
    forward_buf = jnp.zeros((rows_total, D), jnp.bfloat16).at[position].set(token_rows)
    upstream = cotangent.astype(jnp.float32) * predicted[..., None].astype(jnp.float32)
    gate_f32 = gate_probs.reshape(block_count * FTOK, TOPK)
    scaled = (gate_f32[:, :, None] * upstream.reshape(block_count * FTOK, 1, D)).astype(jnp.bfloat16)
    backward_buf = jnp.zeros((rows_total, D), jnp.bfloat16).at[position].set(scaled.reshape(block_count * pair_count, D))
    frame_rows = CLIPS * CAP

    def run_expert(inputs):
        slots_in, slots_grad, up_mat, down_mat = inputs
        preact = jnp.dot(slots_in, up_mat, preferred_element_type=jnp.float32)
        activated = gelu_value(preact).astype(jnp.bfloat16)
        expert_out = jnp.dot(activated, down_mat, preferred_element_type=jnp.float32).astype(jnp.bfloat16)
        grad_act = jnp.dot(slots_grad, down_mat.T, preferred_element_type=jnp.float32)
        grad_pre = (grad_act * gelu_slope(preact)).astype(jnp.bfloat16)
        grad_slots = jnp.dot(grad_pre, up_mat.T, preferred_element_type=jnp.float32).astype(jnp.bfloat16)
        up_part = jnp.einsum('fsd,fsk->fdk', slots_in.reshape(FRAMES, frame_rows, D).astype(jnp.float32), grad_pre.reshape(FRAMES, frame_rows, FF).astype(jnp.float32))
        down_part = jnp.einsum('fsk,fsd->fkd', activated.reshape(FRAMES, frame_rows, FF).astype(jnp.float32), slots_grad.reshape(FRAMES, frame_rows, D).astype(jnp.float32))
        up_part = lax.optimization_barrier(up_part.astype(jnp.bfloat16)).astype(jnp.float32)
        down_part = lax.optimization_barrier(down_part.astype(jnp.bfloat16)).astype(jnp.float32)
        return (expert_out, grad_slots, lax.optimization_barrier(jnp.sum(up_part, 0)).astype(jnp.bfloat16), lax.optimization_barrier(jnp.sum(down_part, 0)).astype(jnp.bfloat16))
    outs_buf, grads_buf, up_grad, down_grad = lax.map(run_expert, (forward_buf.reshape(EXPERTS, -1, D), backward_buf.reshape(EXPERTS, -1, D), up_weight, down_weight))
    outs_buf = lax.optimization_barrier(outs_buf)
    grads_buf = lax.optimization_barrier(grads_buf)
    picked = outs_buf.reshape(rows_total, D)[position].astype(jnp.float32).reshape(block_count * FTOK, TOPK, D)
    mixture = lax.optimization_barrier(jnp.sum(gate_f32[:, :, None] * picked, 1))
    layer_out = (stream_f32.reshape(-1, D) + mixture).astype(jnp.bfloat16).reshape(tokens.shape)
    norm_back = lax.optimization_barrier(jnp.sum(grads_buf.reshape(rows_total, D)[position].astype(jnp.float32).reshape(block_count * FTOK, TOPK, D), 1))
    scaled_back = norm_back * norm_gain
    unit_flat = unit_rows.reshape(-1, D)
    inv_flat = inv_rms.reshape(-1, 1)
    stream_grad = upstream.reshape(-1, D) + inv_flat * (scaled_back - unit_flat * lax.optimization_barrier(jnp.mean(scaled_back * unit_flat, -1, keepdims=True)))
    return (layer_out, stream_grad.astype(jnp.bfloat16).reshape(tokens.shape), up_grad, down_grad)
```

```python
import functools

import jax
import jax.numpy as jnp
from jax import lax
from jax.experimental import pallas as pl
from jax.experimental.pallas import tpu as pltpu
from jax.sharding import PartitionSpec as P

MESH = pl.DeviceIdType.MESH
PEERS = 16
HEADS = 16
HD = 128
D = 2048
FF = 1024
ACTIONS = 64
TOK = 128
CHIPS = 8
BODY = 16
REST = 4
ROWS = 320
PADDED = 384
QUARTER = 512
BLOCK = D + QUARTER

norm_eps = 1e-06
gelu_coef = 0.7978845608028654

f32 = jnp.float32
bf16 = jnp.bfloat16


def dot(a, b):
    return jnp.dot(a, b, preferred_element_type=f32)


def dot_nt(a, b):
    return lax.dot_general(a, b, (((1,), (1,)), ((), ())), preferred_element_type=f32)


def iota(shape, dim):
    return lax.broadcasted_iota(jnp.int32, shape, dim)


def one_hot(mask):
    return mask.astype(f32).astype(bf16)


def tm_peer(me, o):
    return lax.rem(me + o, PEERS)


def expert_peer(me, o):
    y, x = me // 4, lax.rem(me, 4)
    return lax.rem(y + o // 4, 4) * 4 + lax.rem(x + lax.rem(o, 4), 4)


def far_first(s):
    half = s // 2
    return 8 + half - 2 * half * lax.rem(s, 2)


def remote(src, dst, send, recv, axis, peer):
    return pltpu.make_async_remote_copy(
        src_ref=src,
        dst_ref=dst,
        send_sem=send,
        recv_sem=recv,
        device_id={axis: peer},
        device_id_type=MESH,
    )


def each(lo, hi, fn):
    def body(s, c):
        fn(s)
        return c

    lax.fori_loop(lo, hi, body, 0)


def rows_of(p):
    return pl.ds(pl.multiple_of(p * BODY, BODY), BODY)


def exchange_start(src, dst, send, recv, own, me):
    def go(o):
        p = expert_peer(me, o)
        remote(
            src.at[rows_of(p), :], dst.at[rows_of(me), :], send.at[p], recv.at[me], "expert", p
        ).start()

    each(1, PEERS, go)
    pltpu.make_async_copy(src.at[rows_of(me), :], dst.at[rows_of(me), :], own).start()


def exchange_wait(src, dst, send, recv, own, me):
    pltpu.make_async_copy(src.at[rows_of(me), :], dst.at[rows_of(me), :], own).wait()

    def go(o):
        p = expert_peer(me, o)
        remote(
            src.at[rows_of(p), :], dst.at[rows_of(p), :], send.at[p], recv.at[p], "expert", p
        ).wait_recv()

    each(1, PEERS, go)


def exchange_sent(src, dst, send, recv, me):
    def go(o):
        p = expert_peer(me, o)
        remote(
            src.at[rows_of(p), :], dst.at[rows_of(p), :], send.at[p], recv.at[p], "expert", p
        ).wait_send()

    each(1, PEERS, go)


def pack(dst, body_hot, rest_hot, src):
    rest = None
    for q in range(4):
        part = src[:, q * QUARTER : (q + 1) * QUARTER]
        dst[:, q * QUARTER : (q + 1) * QUARTER] = dot(body_hot[...], part).astype(bf16)
        more = dot(rest_hot[q], part)
        rest = more if rest is None else rest + more
    dst[:, D:BLOCK] = rest.astype(bf16)


def rest_pick(q):
    i, j = iota((64, 256), 0), iota((64, 256), 1)
    return one_hot(j == (i // REST) * BODY + q * REST + lax.rem(i, REST))


def rest_put(q):
    j, i = iota((256, 64), 0), iota((256, 64), 1)
    return one_hot(j == (i // REST) * BODY + q * REST + lax.rem(i, REST))


def unpack(dst, src):
    dst[0:256, :] = src[:, 0:D]
    for q in range(4):
        dst[256:ROWS, q * QUARTER : (q + 1) * QUARTER] = dot(rest_pick(q), src[:, D:BLOCK]).astype(
            bf16
        )
    dst[ROWS:PADDED, :] = jnp.zeros((PADDED - ROWS, D), bf16)


def route_hots(routes, body_t, rest_t, body_k, rest_k):
    lane, row = iota((TOK, TOK), 1), iota((TOK, TOK), 0)
    r = routes[...]
    hit = [lane == r[:, k : k + 1] for k in range(2)]
    hits = one_hot(jnp.logical_or(hit[0], hit[1]))
    rank = dot(one_hot(lane < row), hits)
    for k in range(2):
        mine = jnp.sum(jnp.where(hit[k], rank, 0.0), axis=1, keepdims=True)
        base = r[:, k : k + 1].astype(f32) * BODY + mine
        at_body = jnp.where(mine < BODY, base, -1.0)
        at_rest = jnp.where(mine < BODY, -1000.0, base - BODY)
        wide_body = jnp.broadcast_to(at_body, (TOK, TOK))
        wide_rest = jnp.broadcast_to(at_rest, (TOK, TOK))
        slot = iota((TOK, 256), 1).astype(f32)
        body_k[k] = one_hot(slot == jnp.broadcast_to(at_body, (TOK, 256)))
        for q in range(4):
            rest_k[k, q] = one_hot(slot == jnp.broadcast_to(at_rest, (TOK, 256)) + REST * q)
        turned_body, turned_rest = jnp.transpose(wide_body), jnp.transpose(wide_rest)
        for half in range(2):
            rows = slice(half * TOK, (half + 1) * TOK)
            here = (row + half * TOK).astype(f32)
            body_t[rows, k * TOK : (k + 1) * TOK] = one_hot(here == turned_body)
            for q in range(4):
                rest_t[q, rows, k * TOK : (k + 1) * TOK] = one_hot(here == turned_rest + REST * q)


def attend_pair(i, qs, ks, vs, out):
    scale = HD**-0.5
    q = qs[2 * i : 2 * i + 2].reshape(2 * TOK, HD)
    near = dot_nt(q, ks[2 * i : 2 * i + 2].reshape(2 * TOK, HD))
    seen = iota((2 * TOK, 2 * TOK), 1) // TOK <= iota((2 * TOK, 2 * TOK), 0) // TOK
    near = jnp.where(seen, near, -1e30)
    top = jnp.max(near, axis=1, keepdims=True)
    if i:
        far = dot_nt(q, ks[0 : 2 * i].reshape(2 * i * TOK, HD))
        top = jnp.maximum(top, jnp.max(far, axis=1, keepdims=True))
    near = jnp.exp((near - top) * scale)
    total = jnp.sum(near, axis=1, keepdims=True)
    acc = dot(near.astype(bf16), vs[2 * i : 2 * i + 2].reshape(2 * TOK, HD))
    if i:
        far = jnp.exp((far - top) * scale)
        total = total + jnp.sum(far, axis=1, keepdims=True)
        acc = acc + dot(far.astype(bf16), vs[0 : 2 * i].reshape(2 * i * TOK, HD))
    out[2 * i : 2 * i + 2] = (acc / total).astype(bf16).reshape(2, TOK, HD)


def layer_kernel(
    tok,
    cot,
    action,
    table,
    gain,
    routes,
    gates,
    predicted,
    q_any,
    k_any,
    v_any,
    up_any,
    down_any,
    layer_out,
    stream_grad,
    up_grad,
    down_grad,
    up_w,
    down_w,
    qs,
    ks,
    vs,
    heads_out,
    attended,
    stream,
    rows,
    body_t,
    rest_t,
    body_k,
    rest_k,
    grad_send,
    grad_in,
    norm_send,
    norm_in,
    out_send,
    out_in,
    back_send,
    back_in,
    xs,
    gs,
    turned,
    act,
    act_t,
    grad_act,
    grad_pre,
    scaled_back,
    down_part,
    up_part,
    down_pair,
    up_pair,
    down_right,
    down_left,
    up_right,
    up_left,
    w_sem,
    own_sem,
    qkv_own,
    qkv_send,
    qkv_recv,
    o_send,
    o_recv,
    x_send,
    x_recv,
    pair_send,
    pair_recv,
    ring_send,
    ring_recv,
):
    tm, ex = lax.axis_index("tm"), lax.axis_index("expert")
    chip, core = tm // 2, lax.rem(tm, 2)
    sibling = tm + 1 - 2 * core
    right, left = lax.rem(tm + 2, PEERS), lax.rem(tm + PEERS - 2, PEERS)

    up_load = pltpu.make_async_copy(up_any, up_w, w_sem.at[0])
    down_load = pltpu.make_async_copy(down_any, down_w, w_sem.at[1])
    up_load.start()
    down_load.start()

    def columns(p):
        return pl.ds(pl.multiple_of(p * HD, HD), HD)

    trio = ((q_any, qs), (k_any, ks), (v_any, vs))
    own_heads = [
        pltpu.make_async_copy(a.at[:, columns(tm)], b.at[tm], qkv_own.at[n])
        for n, (a, b) in enumerate(trio)
    ]
    for copy in own_heads:
        copy.start()

    barrier = pltpu.get_barrier_semaphore()

    def greet(o):
        pl.semaphore_signal(
            barrier, inc=1, device_id={"tm": tm_peer(tm, o)}, device_id_type=MESH
        )
        pl.semaphore_signal(
            barrier, inc=1, device_id={"expert": expert_peer(ex, o)}, device_id_type=MESH
        )

    each(1, PEERS, greet)
    pl.semaphore_wait(barrier, 2 * (PEERS - 1))

    def send_heads(s):
        p = tm_peer(tm, far_first(s))
        for n, (a, b) in enumerate(trio):
            remote(
                a.at[:, columns(p)], b.at[tm], qkv_send.at[n, p], qkv_recv.at[n, tm], "tm", p
            ).start()

    each(1, PEERS, send_heads)

    route_hots(routes, body_t, rest_t, body_k, rest_k)
    kept = jnp.transpose(jnp.broadcast_to(predicted[...].astype(f32), (TOK, TOK)))[:, 0:1]
    upstream = cot[...].astype(f32) * kept
    for k in range(2):
        rows[k * TOK : (k + 1) * TOK, :] = (gates[:, k : k + 1] * upstream).astype(bf16)
    pack(grad_send, body_t, rest_t, rows)
    exchange_start(grad_send, grad_in, x_send.at[0], x_recv.at[0], own_sem.at[0], ex)

    down_load.wait()
    exchange_wait(grad_in, grad_in, x_send.at[0], x_recv.at[0], own_sem.at[0], ex)
    unpack(gs, grad_in)

    def act_back(n):
        f = pl.ds(pl.multiple_of(n * 256, 256), 256)
        grad_act[:, f] = dot_nt(gs[0:ROWS, :], down_w[f, :])

    each(0, FF // 256, act_back)

    for copy in own_heads:
        copy.wait()

    def wait_heads(o):
        p = tm_peer(tm, o)
        for n, (a, b) in enumerate(trio):
            remote(
                a.at[:, columns(p)], b.at[p], qkv_send.at[n, p], qkv_recv.at[n, p], "tm", p
            ).wait_recv()

    each(1, PEERS, wait_heads)

    def send_attended(p):
        remote(
            heads_out.at[p], attended.at[:, columns(tm)], o_send.at[p], o_recv.at[tm], "tm", p
        ).start()

    def attend(s):
        half = (s + 1) // 2
        i = lax.rem(chip + 4 + half - 2 * half * lax.rem(s, 2), CHIPS)
        lax.switch(
            i,
            [functools.partial(attend_pair, n, qs, ks, vs, heads_out) for n in range(CHIPS)],
        )
        for c in range(2):
            p = 2 * i + c

            @pl.when(p != tm)
            def _():
                send_attended(p)

    each(0, CHIPS, attend)
    own_out = pltpu.make_async_copy(
        heads_out.at[tm], attended.at[:, columns(tm)], own_sem.at[4]
    )
    own_out.start()
    choose = one_hot(iota((8, ACTIONS), 1) == jnp.broadcast_to(action[...], (8, ACTIONS)))
    action_row = dot(choose, table[...])[0:1, :]
    own_out.wait()

    def wait_attended(o):
        p = tm_peer(tm, o)
        remote(
            heads_out.at[p], attended.at[:, columns(p)], o_send.at[p], o_recv.at[p], "tm", p
        ).wait_recv()

    each(1, PEERS, wait_attended)

    total = tok[...].astype(f32) + attended[...].astype(f32) + action_row
    stream[...] = total.astype(bf16)
    held = stream[...].astype(f32)
    inv_rms = lax.rsqrt(jnp.mean(held * held, axis=1, keepdims=True) + norm_eps)
    normed = (held * inv_rms * gain[...]).astype(bf16)
    rows[0:TOK, :] = normed
    rows[TOK : 2 * TOK, :] = normed
    pack(norm_send, body_t, rest_t, rows)
    exchange_start(norm_send, norm_in, x_send.at[1], x_recv.at[1], own_sem.at[1], ex)
    up_load.wait()
    exchange_wait(norm_send, norm_in, x_send.at[1], x_recv.at[1], own_sem.at[1], ex)
    unpack(xs, norm_in)

    act[ROWS:PADDED, :] = jnp.zeros((PADDED - ROWS, FF), bf16)
    grad_pre[ROWS:PADDED, :] = jnp.zeros((PADDED - ROWS, FF), bf16)

    def expert_up(n):
        f = pl.ds(pl.multiple_of(n * 256, 256), 256)
        v = dot(xs[0:ROWS, :], up_w[:, f])
        th = jnp.tanh(gelu_coef * (v + 0.044715 * v * v * v))
        act[0:ROWS, f] = (0.5 * v * (1.0 + th)).astype(bf16)
        slope = 0.5 * (1.0 + th) + 0.5 * v * (1.0 - th * th) * gelu_coef * (
            1.0 + 3.0 * 0.044715 * v * v
        )
        grad_pre[0:ROWS, f] = (grad_act[:, f] * slope).astype(bf16)
        act_t[f, :] = jnp.transpose(act[:, f])

    each(0, FF // 256, expert_up)

    def down_weights(n):
        d = pl.ds(pl.multiple_of(n * 512, 512), 512)
        down_part[:, :, :, d] = dot(act_t[...], gs[:, d]).astype(bf16).reshape(CHIPS, 2, 64, 512)

    each(0, D // 512, down_weights)
    pair_down = remote(
        down_part.at[:, 1 - core], down_pair, pair_send.at[0], pair_recv.at[0], "tm", sibling
    )
    pair_down.start()

    def up_weights(n):
        d = pl.ds(pl.multiple_of(n * 512, 512), 512)
        turned[...] = jnp.transpose(xs[:, d])
        part = dot(turned[...], grad_pre[...]).astype(bf16)
        up_part[pl.ds(n * 2, 2)] = part.reshape(2, 2, 128, FF)

    each(0, D // 512, up_weights)
    pair_up = remote(
        up_part.at[:, 1 - core], up_pair, pair_send.at[1], pair_recv.at[1], "tm", sibling
    )
    pair_up.start()

    def send_rows(dst, product):
        rest = None
        for q in range(4):
            part = product(q).astype(bf16)
            dst[:, q * QUARTER : (q + 1) * QUARTER] = part[0:256, :]
            more = dot(rest_put(q), part[256:ROWS, :])
            rest = more if rest is None else rest + more
        dst[:, D:BLOCK] = rest.astype(bf16)

    send_rows(
        out_send, lambda q: dot(act[0:ROWS, :], down_w[:, q * QUARTER : (q + 1) * QUARTER])
    )
    exchange_start(out_send, out_in, x_send.at[2], x_recv.at[2], own_sem.at[2], ex)

    streams = (
        (down_pair, down_part, down_right, 0, 32, 1, right),
        (down_pair, down_part, down_left, 32, 32, -1, left),
        (up_pair, up_part, up_right, 0, 64, 1, right),
        (up_pair, up_part, up_left, 64, 64, -1, left),
    )

    def chip_sum(n, t):
        pair, part, _, lo, size, _, _ = streams[n]
        return (
            pair[t, lo : lo + size, :].astype(f32) + part[t, core, lo : lo + size, :].astype(f32)
        )

    def hop(n, src, s):
        _, _, slots, _, _, _, to = streams[n]
        return remote(src, slots.at[s], ring_send.at[n, s], ring_recv.at[n, s], "tm", to)

    def first_hop(n):
        pair, _, _, lo, size, way, _ = streams[n]
        t = lax.rem(chip - way + CHIPS, CHIPS)
        pair[t, lo : lo + size, :] = chip_sum(n, t).astype(bf16)
        hop(n, pair.at[t, lo : lo + size, :], 0).start()

    pair_down.wait_recv()
    first_hop(0)
    first_hop(1)
    pair_up.wait_recv()
    first_hop(2)
    first_hop(3)

    send_rows(
        back_send, lambda q: dot_nt(grad_pre[0:ROWS, :], up_w[q * QUARTER : (q + 1) * QUARTER, :])
    )
    exchange_start(back_send, back_in, x_send.at[3], x_recv.at[3], own_sem.at[3], ex)

    def next_hop(s):
        for n, (_, _, slots, _, _, way, _) in enumerate(streams):
            t = lax.rem(chip - way * (1 + s) + 2 * CHIPS, CHIPS)
            hop(n, slots.at[s - 1], s - 1).wait_recv()
            slots[s - 1] = (slots[s - 1].astype(f32) + chip_sum(n, t)).astype(bf16)
            hop(n, slots.at[s - 1], s).start()

    each(1, CHIPS - 1, next_hop)

    exchange_wait(out_send, out_in, x_send.at[2], x_recv.at[2], own_sem.at[2], ex)
    for q in range(4):
        d = slice(q * QUARTER, (q + 1) * QUARTER)
        mixed = stream[:, d].astype(f32)
        for k in range(2):
            picked = dot(body_k[k], out_in[:, d]) + dot(rest_k[k, q], out_in[:, D:BLOCK])
            mixed = mixed + gates[:, k : k + 1] * picked
        layer_out[:, d] = mixed.astype(bf16)

    exchange_wait(back_send, back_in, x_send.at[3], x_recv.at[3], own_sem.at[3], ex)
    held = stream[...].astype(f32)
    inv_rms = lax.rsqrt(jnp.mean(held * held, axis=1, keepdims=True) + norm_eps)
    both = jnp.zeros((TOK, 1), f32)
    for q in range(4):
        d = slice(q * QUARTER, (q + 1) * QUARTER)
        back = dot(body_k[0] + body_k[1], back_in[:, d]) + dot(
            rest_k[0, q] + rest_k[1, q], back_in[:, D:BLOCK]
        )
        back = back * gain[:, d]
        scaled_back[:, d] = back
        unit = stream[:, d].astype(f32) * inv_rms
        both = both + jnp.sum(back * unit, axis=1, keepdims=True)
    both = both * (1.0 / D)
    for q in range(4):
        d = slice(q * QUARTER, (q + 1) * QUARTER)
        unit = stream[:, d].astype(f32) * inv_rms
        up_here = cot[:, d].astype(f32) * kept
        stream_grad[:, d] = (up_here + inv_rms * (scaled_back[:, d] - unit * both)).astype(bf16)

    for n, out in ((0, down_grad), (1, down_grad), (2, up_grad), (3, up_grad)):
        _, _, slots, lo, size, _, _ = streams[n]
        hop(n, slots.at[CHIPS - 2], CHIPS - 2).wait_recv()
        out[lo : lo + size, :] = (slots[CHIPS - 2].astype(f32) + chip_sum(n, chip)).astype(bf16)

    def sent(o):
        p = tm_peer(tm, o)
        for n, (a, b) in enumerate(trio):
            remote(
                a.at[:, columns(p)], b.at[p], qkv_send.at[n, p], qkv_recv.at[n, p], "tm", p
            ).wait_send()
        remote(
            heads_out.at[p], attended.at[:, columns(p)], o_send.at[p], o_recv.at[p], "tm", p
        ).wait_send()

    each(1, PEERS, sent)
    for n, (a, b) in enumerate(
        ((grad_send, grad_in), (norm_send, norm_in), (out_send, out_in), (back_send, back_in))
    ):
        exchange_sent(a, b, x_send.at[n], x_recv.at[n], ex)
    pair_down.wait_send()
    pair_up.wait_send()

    def hops_sent(s):
        for n, (_, _, slots, _, _, _, _) in enumerate(streams):
            hop(n, slots.at[s], s).wait_send()

    each(0, CHIPS - 1, hops_sent)


def local(
    tokens,
    queries,
    key_rows,
    values,
    actions,
    action_table,
    norm_gain,
    routes,
    gate_probs,
    predicted,
    cotangent,
    up_weight,
    down_weight,
):
    vmem = pl.BlockSpec(memory_space=pltpu.VMEM)
    hbm = pl.BlockSpec(memory_space=pl.ANY)
    dma = pltpu.SemaphoreType.DMA
    block = pltpu.VMEM((256, BLOCK), bf16)
    head = pltpu.VMEM((PEERS, TOK, HD), bf16)
    layer_out, stream_grad, up_grad, down_grad = pl.pallas_call(
        layer_kernel,
        out_shape=(
            jax.ShapeDtypeStruct((TOK, D), bf16),
            jax.ShapeDtypeStruct((TOK, D), bf16),
            jax.ShapeDtypeStruct((D // PEERS, FF), bf16),
            jax.ShapeDtypeStruct((FF // PEERS, D), bf16),
        ),
        in_specs=[vmem] * 8 + [hbm] * 5,
        out_specs=(vmem,) * 4,
        scratch_shapes=[
            pltpu.VMEM((D, FF), bf16),
            pltpu.VMEM((FF, D), bf16),
            head,
            head,
            head,
            head,
            pltpu.VMEM((TOK, D), bf16),
            pltpu.VMEM((TOK, D), bf16),
            pltpu.VMEM((2 * TOK, D), bf16),
            pltpu.VMEM((256, 256), bf16),
            pltpu.VMEM((4, 256, 256), bf16),
            pltpu.VMEM((2, TOK, 256), bf16),
            pltpu.VMEM((2, 4, TOK, 256), bf16),
        ]
        + [block] * 8
        + [
            pltpu.VMEM((PADDED, D), bf16),
            pltpu.VMEM((PADDED, D), bf16),
            pltpu.VMEM((512, PADDED), bf16),
            pltpu.VMEM((PADDED, FF), bf16),
            pltpu.VMEM((FF, PADDED), bf16),
            pltpu.VMEM((ROWS, FF), f32),
            pltpu.VMEM((PADDED, FF), bf16),
            pltpu.VMEM((TOK, D), f32),
            pltpu.VMEM((CHIPS, 2, 64, D), bf16),
            pltpu.VMEM((CHIPS, 2, 128, FF), bf16),
            pltpu.VMEM((CHIPS, 64, D), bf16),
            pltpu.VMEM((CHIPS, 128, FF), bf16),
            pltpu.VMEM((CHIPS - 1, 32, D), bf16),
            pltpu.VMEM((CHIPS - 1, 32, D), bf16),
            pltpu.VMEM((CHIPS - 1, 64, FF), bf16),
            pltpu.VMEM((CHIPS - 1, 64, FF), bf16),
            dma((2,)),
            dma((5,)),
            dma((3,)),
            dma((3, PEERS)),
            dma((3, PEERS)),
            dma((PEERS,)),
            dma((PEERS,)),
            dma((4, PEERS)),
            dma((4, PEERS)),
            dma((2,)),
            dma((2,)),
            dma((4, CHIPS - 1)),
            dma((4, CHIPS - 1)),
        ],
        compiler_params=pltpu.CompilerParams(
            collective_id=0, has_side_effects=True, vmem_limit_bytes=62 * 2**20
        ),
        name="layer",
    )(
        tokens.reshape(TOK, D),
        cotangent.reshape(TOK, D),
        actions,
        action_table,
        norm_gain.reshape(1, D),
        routes.reshape(TOK, 2),
        gate_probs.reshape(TOK, 2),
        predicted.reshape(1, TOK),
        queries.reshape(TOK, D),
        key_rows.reshape(TOK, D),
        values.reshape(TOK, D),
        up_weight.reshape(D, FF),
        down_weight.reshape(FF, D),
    )
    return (
        layer_out.reshape(tokens.shape),
        stream_grad.reshape(tokens.shape),
        up_grad.reshape(1, D // PEERS, FF),
        down_grad.reshape(1, FF // PEERS, D),
    )


def solution(mesh):
    rows = P("expert", "tm", None, None)
    in_specs = (
        rows,
        rows,
        rows,
        rows,
        P("expert", "tm"),
        P(),
        P(),
        rows,
        rows,
        P("expert", "tm", None),
        rows,
        P("expert", None, None),
        P("expert", None, None),
    )
    out_specs = (rows, rows, P("expert", "tm", None), P("expert", "tm", None))
    return jax.shard_map(local, mesh=mesh, in_specs=in_specs, out_specs=out_specs, check_vma=False)
```

```python
import functools

import jax
import jax.numpy as jnp
from jax import lax
from jax.experimental import pallas as pl
from jax.experimental.pallas import tpu as pltpu
from jax.sharding import PartitionSpec as P

MESH = pl.DeviceIdType.MESH
PEERS = 16
HEADS = 16
HD = 128
D = 2048
FF = 1024
ACTIONS = 64
TOK = 128
CHIPS = 8
BODY = 16
REST = 4
ROWS = 320
PADDED = 384
QUARTER = 512
BLOCK = D + QUARTER

norm_eps = 1e-06
gelu_coef = 0.7978845608028654

f32 = jnp.float32
bf16 = jnp.bfloat16


def dot(a, b):
    return jnp.dot(a, b, preferred_element_type=f32)


def dot_nt(a, b):
    return lax.dot_general(a, b, (((1,), (1,)), ((), ())), preferred_element_type=f32)


def iota(shape, dim):
    return lax.broadcasted_iota(jnp.int32, shape, dim)


def one_hot(mask):
    return mask.astype(f32).astype(bf16)


def tm_peer(me, o):
    return lax.rem(me + o, PEERS)


def expert_peer(me, o):
    y, x = me // 4, lax.rem(me, 4)
    return lax.rem(y + o // 4, 4) * 4 + lax.rem(x + lax.rem(o, 4), 4)


FAR_FIRST = (10, 2, 8, 6, 14, 9, 11, 5, 7, 13, 15, 1, 3, 4, 12)


def far_first(s):
    half = s // 2
    return 8 + half - 2 * half * lax.rem(s, 2)


def remote(src, dst, send, recv, axis, peer):
    return pltpu.make_async_remote_copy(
        src_ref=src,
        dst_ref=dst,
        send_sem=send,
        recv_sem=recv,
        device_id={axis: peer},
        device_id_type=MESH,
    )


def each(lo, hi, fn):
    def body(s, c):
        fn(s)
        return c

    lax.fori_loop(lo, hi, body, 0)


def rows_of(p):
    return pl.ds(pl.multiple_of(p * BODY, BODY), BODY)


def exchange_start(src, dst, send, recv, own, me):
    def go(o):
        p = expert_peer(me, o)
        remote(
            src.at[rows_of(p), :], dst.at[rows_of(me), :], send.at[p], recv.at[me], "expert", p
        ).start()

    for o in FAR_FIRST:
        go(o)
    pltpu.make_async_copy(src.at[rows_of(me), :], dst.at[rows_of(me), :], own).start()


def exchange_wait(src, dst, send, recv, own, me):
    pltpu.make_async_copy(src.at[rows_of(me), :], dst.at[rows_of(me), :], own).wait()

    def go(o):
        p = expert_peer(me, o)
        remote(
            src.at[rows_of(p), :], dst.at[rows_of(p), :], send.at[p], recv.at[p], "expert", p
        ).wait_recv()

    each(1, PEERS, go)


def exchange_sent(src, dst, send, recv, me):
    def go(o):
        p = expert_peer(me, o)
        remote(
            src.at[rows_of(p), :], dst.at[rows_of(p), :], send.at[p], recv.at[p], "expert", p
        ).wait_send()

    each(1, PEERS, go)


def pack(dst, body_hot, rest_hot, src):
    rest = None
    for q in range(4):
        part = src[:, q * QUARTER : (q + 1) * QUARTER]
        dst[:, q * QUARTER : (q + 1) * QUARTER] = dot(body_hot[...], part).astype(bf16)
        more = dot(rest_hot[q], part)
        rest = more if rest is None else rest + more
    dst[:, D:BLOCK] = rest.astype(bf16)


def rest_pick(q):
    i, j = iota((64, 256), 0), iota((64, 256), 1)
    return one_hot(j == (i // REST) * BODY + q * REST + lax.rem(i, REST))


def rest_put(q):
    j, i = iota((256, 64), 0), iota((256, 64), 1)
    return one_hot(j == (i // REST) * BODY + q * REST + lax.rem(i, REST))


def unpack(dst, src):
    dst[0:256, :] = src[:, 0:D]
    for q in range(4):
        dst[256:ROWS, q * QUARTER : (q + 1) * QUARTER] = dot(rest_pick(q), src[:, D:BLOCK]).astype(
            bf16
        )
    dst[ROWS:PADDED, :] = jnp.zeros((PADDED - ROWS, D), bf16)


def turned_row(ref, k):
    return jnp.transpose(jnp.broadcast_to(ref[k : k + 1, :].astype(f32), (TOK, TOK)))


def route_hots(routes, body_t, rest_t, body_k, rest_k):
    lane, row = iota((TOK, TOK), 1), iota((TOK, TOK), 0)
    r = [turned_row(routes, k) for k in range(2)]
    hit = [lane.astype(f32) == r[k] for k in range(2)]
    hits = one_hot(jnp.logical_or(hit[0], hit[1]))
    rank = dot(one_hot(lane < row), hits)
    for k in range(2):
        mine = jnp.sum(jnp.where(hit[k], rank, 0.0), axis=1, keepdims=True)
        base = r[k][:, 0:1] * BODY + mine
        at_body = jnp.where(mine < BODY, base, -1.0)
        at_rest = jnp.where(mine < BODY, -1000.0, base - BODY)
        wide_body = jnp.broadcast_to(at_body, (TOK, TOK))
        wide_rest = jnp.broadcast_to(at_rest, (TOK, TOK))
        slot = iota((TOK, 256), 1).astype(f32)
        body_k[k] = one_hot(slot == jnp.broadcast_to(at_body, (TOK, 256)))
        for q in range(4):
            rest_k[k, q] = one_hot(slot == jnp.broadcast_to(at_rest, (TOK, 256)) + REST * q)
        turned_body, turned_rest = jnp.transpose(wide_body), jnp.transpose(wide_rest)
        for half in range(2):
            rows = slice(half * TOK, (half + 1) * TOK)
            here = (row + half * TOK).astype(f32)
            body_t[rows, k * TOK : (k + 1) * TOK] = one_hot(here == turned_body)
            for q in range(4):
                rest_t[q, rows, k * TOK : (k + 1) * TOK] = one_hot(here == turned_rest + REST * q)


def attend_pair(i, qs, ks, vs, out):
    scale = HD**-0.5
    q = qs[2 * i : 2 * i + 2].reshape(2 * TOK, HD)
    near = dot_nt(q, ks[2 * i : 2 * i + 2].reshape(2 * TOK, HD))
    seen = iota((2 * TOK, 2 * TOK), 1) // TOK <= iota((2 * TOK, 2 * TOK), 0) // TOK
    near = jnp.where(seen, near, -1e30)
    top = jnp.max(near, axis=1, keepdims=True)
    if i:
        far = dot_nt(q, ks[0 : 2 * i].reshape(2 * i * TOK, HD))
        top = jnp.maximum(top, jnp.max(far, axis=1, keepdims=True))
    near = jnp.exp((near - top) * scale)
    total = jnp.sum(near, axis=1, keepdims=True)
    acc = dot(near.astype(bf16), vs[2 * i : 2 * i + 2].reshape(2 * TOK, HD))
    if i:
        far = jnp.exp((far - top) * scale)
        total = total + jnp.sum(far, axis=1, keepdims=True)
        acc = acc + dot(far.astype(bf16), vs[0 : 2 * i].reshape(2 * i * TOK, HD))
    out[2 * i : 2 * i + 2] = (acc / total).astype(bf16).reshape(2, TOK, HD)


def layer_kernel(
    tok_any,
    cot_any,
    action_any,
    table_any,
    gain_any,
    routes_any,
    gates_any,
    predicted_any,
    q_any,
    k_any,
    v_any,
    up_any,
    down_any,
    layer_any,
    stream_grad_any,
    up_grad_any,
    down_grad_any,
    tok,
    cot,
    action,
    table,
    gain,
    routes,
    gates,
    predicted,
    layer_out,
    stream_grad,
    up_grad,
    down_grad,
    up_w,
    down_w,
    qs,
    ks,
    vs,
    heads_out,
    attended,
    stream,
    rows,
    body_t,
    rest_t,
    body_k,
    rest_k,
    grad_send,
    grad_in,
    norm_send,
    norm_in,
    out_send,
    out_in,
    back_send,
    back_in,
    xs,
    gs,
    turned,
    act,
    act_t,
    grad_act,
    grad_pre,
    scaled_back,
    down_part,
    up_part,
    down_pair,
    up_pair,
    down_right,
    down_left,
    up_right,
    up_left,
    fetch_sem,
    result_sem,
    w_sem,
    own_sem,
    qkv_own,
    qkv_send,
    qkv_recv,
    o_send,
    o_recv,
    x_send,
    x_recv,
    pair_send,
    pair_recv,
    ring_send,
    ring_recv,
):
    tm, ex = lax.axis_index("tm"), lax.axis_index("expert")
    chip, core = tm // 2, lax.rem(tm, 2)
    sibling = tm + 1 - 2 * core
    right, left = lax.rem(tm + 2, PEERS), lax.rem(tm + PEERS - 2, PEERS)

    def fetch(n, src, dst):
        return pltpu.make_async_copy(src, dst, fetch_sem.at[n])

    first = [
        fetch(0, routes_any, routes),
        fetch(1, gates_any, gates),
        fetch(2, predicted_any, predicted),
        fetch(3, cot_any, cot),
    ]
    later = [
        fetch(4, tok_any, tok),
        fetch(5, action_any, action),
        fetch(6, table_any, table),
        fetch(7, gain_any, gain),
    ]
    up_load = pltpu.make_async_copy(up_any, up_w, w_sem.at[0])
    down_load = pltpu.make_async_copy(down_any, down_w, w_sem.at[1])

    def columns(p):
        return pl.ds(pl.multiple_of(p * HD, HD), HD)

    trio = ((q_any, qs), (k_any, ks), (v_any, vs))
    own_heads = [
        pltpu.make_async_copy(a.at[:, columns(tm)], b.at[tm], qkv_own.at[n])
        for n, (a, b) in enumerate(trio)
    ]

    barrier = pltpu.get_barrier_semaphore()

    def greet(o):
        pl.semaphore_signal(
            barrier, inc=1, device_id={"tm": tm_peer(tm, o)}, device_id_type=MESH
        )
        pl.semaphore_signal(
            barrier, inc=1, device_id={"expert": expert_peer(ex, o)}, device_id_type=MESH
        )

    each(1, PEERS, greet)
    for copy in first + own_heads + later + [down_load, up_load]:
        copy.start()

    for copy in first:
        copy.wait()
    route_hots(routes, body_t, rest_t, body_k, rest_k)
    kept = turned_row(predicted, 0)[:, 0:1]
    gate = [turned_row(gates, k)[:, 0:1] for k in range(2)]
    upstream = cot[...].astype(f32) * kept
    for k in range(2):
        rows[k * TOK : (k + 1) * TOK, :] = (gate[k] * upstream).astype(bf16)
    pack(grad_send, body_t, rest_t, rows)

    pl.semaphore_wait(barrier, 2 * (PEERS - 1))

    def send_head(n, s):
        p = tm_peer(tm, far_first(s))
        a, b = trio[n]
        remote(
            a.at[:, columns(p)], b.at[tm], qkv_send.at[n, p], qkv_recv.at[n, tm], "tm", p
        ).start()

    def send_keys(s):
        send_head(1, s)
        send_head(2, s)

    each(1, PEERS, send_keys)
    exchange_start(grad_send, grad_in, x_send.at[0], x_recv.at[0], own_sem.at[0], ex)
    each(1, PEERS, functools.partial(send_head, 0))

    for copy in own_heads:
        copy.wait()

    def wait_head(n, p):
        a, b = trio[n]
        remote(
            a.at[:, columns(p)], b.at[p], qkv_send.at[n, p], qkv_recv.at[n, p], "tm", p
        ).wait_recv()

    def wait_keys(o):
        p = tm_peer(tm, o)
        wait_head(1, p)
        wait_head(2, p)

    each(1, PEERS, wait_keys)

    def send_attended(p):
        remote(
            heads_out.at[p], attended.at[:, columns(tm)], o_send.at[p], o_recv.at[tm], "tm", p
        ).start()

    def attend(s):
        half = (s + 1) // 2
        i = lax.rem(chip + 4 + half - 2 * half * lax.rem(s, 2), CHIPS)
        for c in range(2):
            p = 2 * i + c

            @pl.when(p != tm)
            def _():
                wait_head(0, p)

        lax.switch(
            i,
            [functools.partial(attend_pair, n, qs, ks, vs, heads_out) for n in range(CHIPS)],
        )
        for c in range(2):
            p = 2 * i + c

            @pl.when(p != tm)
            def _():
                send_attended(p)

    each(0, CHIPS, attend)
    own_out = pltpu.make_async_copy(
        heads_out.at[tm], attended.at[:, columns(tm)], own_sem.at[4]
    )
    own_out.start()
    for copy in later:
        copy.wait()
    choose = one_hot(iota((8, ACTIONS), 1) == jnp.broadcast_to(action[...], (8, ACTIONS)))
    action_row = dot(choose, table[...])[0:1, :]
    own_out.wait()

    def wait_attended(o):
        p = tm_peer(tm, o)
        remote(
            heads_out.at[p], attended.at[:, columns(p)], o_send.at[p], o_recv.at[p], "tm", p
        ).wait_recv()

    each(1, PEERS, wait_attended)

    total = tok[...].astype(f32) + attended[...].astype(f32) + action_row
    stream[...] = total.astype(bf16)
    held = stream[...].astype(f32)
    inv_rms = lax.rsqrt(jnp.mean(held * held, axis=1, keepdims=True) + norm_eps)
    normed = (held * inv_rms * gain[...]).astype(bf16)
    rows[0:TOK, :] = normed
    rows[TOK : 2 * TOK, :] = normed
    pack(norm_send, body_t, rest_t, rows)
    exchange_start(norm_send, norm_in, x_send.at[1], x_recv.at[1], own_sem.at[1], ex)

    down_load.wait()
    exchange_wait(grad_send, grad_in, x_send.at[0], x_recv.at[0], own_sem.at[0], ex)
    unpack(gs, grad_in)

    def act_back(n):
        f = pl.ds(pl.multiple_of(n * 256, 256), 256)
        grad_act[:, f] = dot_nt(gs[0:ROWS, :], down_w[f, :])

    each(0, FF // 256, act_back)
    up_load.wait()
    exchange_wait(norm_send, norm_in, x_send.at[1], x_recv.at[1], own_sem.at[1], ex)
    unpack(xs, norm_in)

    act[ROWS:PADDED, :] = jnp.zeros((PADDED - ROWS, FF), bf16)
    grad_pre[ROWS:PADDED, :] = jnp.zeros((PADDED - ROWS, FF), bf16)

    def expert_up(n):
        f = pl.ds(pl.multiple_of(n * 256, 256), 256)
        v = dot(xs[0:ROWS, :], up_w[:, f])
        th = jnp.tanh(gelu_coef * (v + 0.044715 * v * v * v))
        act[0:ROWS, f] = (0.5 * v * (1.0 + th)).astype(bf16)
        slope = 0.5 * (1.0 + th) + 0.5 * v * (1.0 - th * th) * gelu_coef * (
            1.0 + 3.0 * 0.044715 * v * v
        )
        grad_pre[0:ROWS, f] = (grad_act[:, f] * slope).astype(bf16)
        act_t[f, :] = jnp.transpose(act[:, f])

    each(0, FF // 256, expert_up)

    def down_weights(n):
        d = pl.ds(pl.multiple_of(n * 512, 512), 512)
        down_part[:, :, :, d] = dot(act_t[...], gs[:, d]).astype(bf16).reshape(CHIPS, 2, 64, 512)

    each(0, D // 512, down_weights)
    pair_down = remote(
        down_part.at[:, 1 - core], down_pair, pair_send.at[0], pair_recv.at[0], "tm", sibling
    )
    pair_down.start()

    def up_weights(n):
        d = pl.ds(pl.multiple_of(n * 512, 512), 512)
        turned[...] = jnp.transpose(xs[:, d])
        part = dot(turned[...], grad_pre[...]).astype(bf16)
        up_part[pl.ds(n * 2, 2)] = part.reshape(2, 2, 128, FF)

    each(0, D // 512, up_weights)
    pair_up = remote(
        up_part.at[:, 1 - core], up_pair, pair_send.at[1], pair_recv.at[1], "tm", sibling
    )
    pair_up.start()

    def send_rows(dst, product):
        rest = None
        for q in range(4):
            part = product(q).astype(bf16)
            dst[:, q * QUARTER : (q + 1) * QUARTER] = part[0:256, :]
            more = dot(rest_put(q), part[256:ROWS, :])
            rest = more if rest is None else rest + more
        dst[:, D:BLOCK] = rest.astype(bf16)

    streams = (
        (down_pair, down_part, down_right, 0, 32, 1, right),
        (down_pair, down_part, down_left, 32, 32, -1, left),
        (up_pair, up_part, up_right, 0, 64, 1, right),
        (up_pair, up_part, up_left, 64, 64, -1, left),
    )

    def chip_sum(n, t):
        pair, part, _, lo, size, _, _ = streams[n]
        return (
            pair[t, lo : lo + size, :].astype(f32) + part[t, core, lo : lo + size, :].astype(f32)
        )

    def hop(n, src, s):
        _, _, slots, _, _, _, to = streams[n]
        return remote(src, slots.at[s], ring_send.at[n, s], ring_recv.at[n, s], "tm", to)

    def first_hop(n):
        pair, _, _, lo, size, way, _ = streams[n]
        t = lax.rem(chip - way + CHIPS, CHIPS)
        pair[t, lo : lo + size, :] = chip_sum(n, t).astype(bf16)
        hop(n, pair.at[t, lo : lo + size, :], 0).start()

    def next_hop(n, s):
        _, _, slots, _, _, way, _ = streams[n]
        t = lax.rem(chip - way * (1 + s) + 2 * CHIPS, CHIPS)
        hop(n, slots.at[s - 1], s - 1).wait_recv()
        slots[s - 1] = (slots[s - 1].astype(f32) + chip_sum(n, t)).astype(bf16)
        hop(n, slots.at[s - 1], s).start()

    pair_down.wait_recv()
    first_hop(0)
    first_hop(1)
    send_rows(
        out_send, lambda q: dot(act[0:ROWS, :], down_w[:, q * QUARTER : (q + 1) * QUARTER])
    )
    exchange_start(out_send, out_in, x_send.at[2], x_recv.at[2], own_sem.at[2], ex)

    pair_up.wait_recv()
    first_hop(2)
    first_hop(3)
    next_hop(0, 1)
    next_hop(1, 1)

    send_rows(
        back_send, lambda q: dot_nt(grad_pre[0:ROWS, :], up_w[q * QUARTER : (q + 1) * QUARTER, :])
    )
    exchange_start(back_send, back_in, x_send.at[3], x_recv.at[3], own_sem.at[3], ex)

    def hops(s):
        next_hop(2, s)
        next_hop(3, s)
        next_hop(0, s + 1)
        next_hop(1, s + 1)

    each(1, CHIPS - 2, hops)
    next_hop(2, CHIPS - 2)
    next_hop(3, CHIPS - 2)

    exchange_wait(out_send, out_in, x_send.at[2], x_recv.at[2], own_sem.at[2], ex)
    for q in range(4):
        d = slice(q * QUARTER, (q + 1) * QUARTER)
        mixed = stream[:, d].astype(f32)
        for k in range(2):
            picked = dot(body_k[k], out_in[:, d]) + dot(rest_k[k, q], out_in[:, D:BLOCK])
            mixed = mixed + gate[k] * picked
        layer_out[:, d] = mixed.astype(bf16)
    layer_store = pltpu.make_async_copy(layer_out, layer_any, result_sem.at[0])
    layer_store.start()

    exchange_wait(back_send, back_in, x_send.at[3], x_recv.at[3], own_sem.at[3], ex)
    held = stream[...].astype(f32)
    inv_rms = lax.rsqrt(jnp.mean(held * held, axis=1, keepdims=True) + norm_eps)
    both = jnp.zeros((TOK, 1), f32)
    for q in range(4):
        d = slice(q * QUARTER, (q + 1) * QUARTER)
        back = dot(body_k[0] + body_k[1], back_in[:, d]) + dot(
            rest_k[0, q] + rest_k[1, q], back_in[:, D:BLOCK]
        )
        back = back * gain[:, d]
        scaled_back[:, d] = back
        unit = stream[:, d].astype(f32) * inv_rms
        both = both + jnp.sum(back * unit, axis=1, keepdims=True)
    both = both * (1.0 / D)
    for q in range(4):
        d = slice(q * QUARTER, (q + 1) * QUARTER)
        unit = stream[:, d].astype(f32) * inv_rms
        up_here = cot[:, d].astype(f32) * kept
        stream_grad[:, d] = (up_here + inv_rms * (scaled_back[:, d] - unit * both)).astype(bf16)

    stream_store = pltpu.make_async_copy(stream_grad, stream_grad_any, result_sem.at[1])
    stream_store.start()

    def sent(o):
        p = tm_peer(tm, o)
        for n, (a, b) in enumerate(trio):
            remote(
                a.at[:, columns(p)], b.at[p], qkv_send.at[n, p], qkv_recv.at[n, p], "tm", p
            ).wait_send()
        remote(
            heads_out.at[p], attended.at[:, columns(p)], o_send.at[p], o_recv.at[p], "tm", p
        ).wait_send()

    each(1, PEERS, sent)
    for n, (a, b) in enumerate(
        ((grad_send, grad_in), (norm_send, norm_in), (out_send, out_in), (back_send, back_in))
    ):
        exchange_sent(a, b, x_send.at[n], x_recv.at[n], ex)
    for n, out in ((0, down_grad), (1, down_grad), (2, up_grad), (3, up_grad)):
        _, _, slots, lo, size, _, _ = streams[n]
        hop(n, slots.at[CHIPS - 2], CHIPS - 2).wait_recv()
        out[lo : lo + size, :] = (slots[CHIPS - 2].astype(f32) + chip_sum(n, chip)).astype(bf16)

    up_store = pltpu.make_async_copy(up_grad, up_grad_any, result_sem.at[2])
    down_store = pltpu.make_async_copy(down_grad, down_grad_any, result_sem.at[3])
    up_store.start()
    down_store.start()
    pair_down.wait_send()
    pair_up.wait_send()

    def hops_sent(s):
        for n, (_, _, slots, _, _, _, _) in enumerate(streams):
            hop(n, slots.at[s], s).wait_send()

    each(0, CHIPS - 1, hops_sent)
    for copy in (layer_store, stream_store, up_store, down_store):
        copy.wait()


def deliver_kernel(*refs):
    made, given, held, came, left = refs[0:4], refs[4:8], refs[8:12], refs[12], refs[13]
    inward = [pltpu.make_async_copy(made[n], held[n], came.at[n]) for n in range(4)]
    outward = [pltpu.make_async_copy(held[n], given[n], left.at[n]) for n in range(4)]
    for copy in inward:
        copy.start()
    for n in range(4):
        inward[n].wait()
        outward[n].start()
    for copy in outward:
        copy.wait()


def local(
    tokens,
    queries,
    key_rows,
    values,
    actions,
    action_table,
    norm_gain,
    routes,
    gate_probs,
    predicted,
    cotangent,
    up_weight,
    down_weight,
):
    hbm = pl.BlockSpec(memory_space=pl.ANY)
    dma = pltpu.SemaphoreType.DMA
    block = pltpu.VMEM((256, BLOCK), bf16)
    head = pltpu.VMEM((PEERS, TOK, HD), bf16)
    results = (
        jax.ShapeDtypeStruct((TOK, D), bf16),
        jax.ShapeDtypeStruct((TOK, D), bf16),
        jax.ShapeDtypeStruct((D // PEERS, FF), bf16),
        jax.ShapeDtypeStruct((FF // PEERS, D), bf16),
    )
    made = pl.pallas_call(
        layer_kernel,
        out_shape=results,
        in_specs=[hbm] * 13,
        out_specs=(hbm,) * 4,
        scratch_shapes=[
            pltpu.VMEM((TOK, D), bf16),
            pltpu.VMEM((TOK, D), bf16),
            pltpu.VMEM((1, 1), jnp.int32),
            pltpu.VMEM((ACTIONS, D), bf16),
            pltpu.VMEM((1, D), f32),
            pltpu.VMEM((2, TOK), jnp.int32),
            pltpu.VMEM((2, TOK), f32),
            pltpu.VMEM((1, TOK), jnp.int32),
            pltpu.VMEM((TOK, D), bf16),
            pltpu.VMEM((TOK, D), bf16),
            pltpu.VMEM((D // PEERS, FF), bf16),
            pltpu.VMEM((FF // PEERS, D), bf16),
            pltpu.VMEM((D, FF), bf16),
            pltpu.VMEM((FF, D), bf16),
            head,
            head,
            head,
            head,
            pltpu.VMEM((TOK, D), bf16),
            pltpu.VMEM((TOK, D), bf16),
            pltpu.VMEM((2 * TOK, D), bf16),
            pltpu.VMEM((256, 256), bf16),
            pltpu.VMEM((4, 256, 256), bf16),
            pltpu.VMEM((2, TOK, 256), bf16),
            pltpu.VMEM((2, 4, TOK, 256), bf16),
        ]
        + [block] * 8
        + [
            pltpu.VMEM((PADDED, D), bf16),
            pltpu.VMEM((PADDED, D), bf16),
            pltpu.VMEM((512, PADDED), bf16),
            pltpu.VMEM((PADDED, FF), bf16),
            pltpu.VMEM((FF, PADDED), bf16),
            pltpu.VMEM((ROWS, FF), f32),
            pltpu.VMEM((PADDED, FF), bf16),
            pltpu.VMEM((TOK, D), f32),
            pltpu.VMEM((CHIPS, 2, 64, D), bf16),
            pltpu.VMEM((CHIPS, 2, 128, FF), bf16),
            pltpu.VMEM((CHIPS, 64, D), bf16),
            pltpu.VMEM((CHIPS, 128, FF), bf16),
            pltpu.VMEM((CHIPS - 1, 32, D), bf16),
            pltpu.VMEM((CHIPS - 1, 32, D), bf16),
            pltpu.VMEM((CHIPS - 1, 64, FF), bf16),
            pltpu.VMEM((CHIPS - 1, 64, FF), bf16),
            dma((8,)),
            dma((4,)),
            dma((2,)),
            dma((5,)),
            dma((3,)),
            dma((3, PEERS)),
            dma((3, PEERS)),
            dma((PEERS,)),
            dma((PEERS,)),
            dma((4, PEERS)),
            dma((4, PEERS)),
            dma((2,)),
            dma((2,)),
            dma((4, CHIPS - 1)),
            dma((4, CHIPS - 1)),
        ],
        compiler_params=pltpu.CompilerParams(
            collective_id=0, has_side_effects=True, vmem_limit_bytes=62 * 2**20
        ),
        name="layer",
    )(
        tokens.reshape(TOK, D),
        cotangent.reshape(TOK, D),
        actions,
        action_table,
        norm_gain.reshape(1, D),
        routes.reshape(TOK, 2).T,
        gate_probs.reshape(TOK, 2).T,
        predicted.reshape(1, TOK),
        queries.reshape(TOK, D),
        key_rows.reshape(TOK, D),
        values.reshape(TOK, D),
        up_weight.reshape(D, FF),
        down_weight.reshape(FF, D),
    )
    layer_out, stream_grad, up_grad, down_grad = pl.pallas_call(
        deliver_kernel,
        out_shape=results,
        in_specs=[hbm] * 4,
        out_specs=(hbm,) * 4,
        scratch_shapes=[pltpu.VMEM(r.shape, r.dtype) for r in results] + [dma((4,)), dma((4,))],
        name="deliver",
    )(*made)
    return (
        layer_out.reshape(tokens.shape),
        stream_grad.reshape(tokens.shape),
        up_grad.reshape(1, D // PEERS, FF),
        down_grad.reshape(1, FF // PEERS, D),
    )


def solution(mesh):
    rows = P("expert", "tm", None, None)
    in_specs = (
        rows,
        rows,
        rows,
        rows,
        P("expert", "tm"),
        P(),
        P(),
        rows,
        rows,
        P("expert", "tm", None),
        rows,
        P("expert", None, None),
        P("expert", None, None),
    )
    out_specs = (rows, rows, P("expert", "tm", None), P("expert", "tm", None))
    return jax.shard_map(local, mesh=mesh, in_specs=in_specs, out_specs=out_specs, check_vma=False)
```

```python
import functools

import jax
import jax.numpy as jnp
from jax import lax
from jax.experimental import pallas as pl
from jax.experimental.pallas import tpu as pltpu
from jax.sharding import PartitionSpec as P

MESH = pl.DeviceIdType.MESH
PEERS = 16
HEADS = 16
HD = 128
D = 2048
FF = 1024
ACTIONS = 64
TOK = 128
CHIPS = 8
BODY = 16
REST = 4
ROWS = 320
PADDED = 384
QUARTER = 512
BLOCK = D + QUARTER
HALF = D // 2
PIECE = HALF // 4
HALF_BLOCK = HALF + PIECE
PHASES = 2

norm_eps = 1e-06
gelu_coef = 0.7978845608028654

f32 = jnp.float32
bf16 = jnp.bfloat16


def dot(a, b):
    return jnp.dot(a, b, preferred_element_type=f32)


def dot_nt(a, b):
    return lax.dot_general(a, b, (((1,), (1,)), ((), ())), preferred_element_type=f32)


def iota(shape, dim):
    return lax.broadcasted_iota(jnp.int32, shape, dim)


def one_hot(mask):
    return mask.astype(f32).astype(bf16)


def tm_peer(me, o):
    return lax.rem(me + o, PEERS)


def expert_peer(me, o):
    y, x = me // 4, lax.rem(me, 4)
    return lax.rem(y + o // 4, 4) * 4 + lax.rem(x + lax.rem(o, 4), 4)


FAR_FIRST = (10, 2, 8, 6, 14, 9, 11, 5, 7, 13, 15, 1, 3, 4, 12)


def far_first(s):
    half = s // 2
    return 8 + half - 2 * half * lax.rem(s, 2)


def remote(src, dst, send, recv, axis, peer):
    return pltpu.make_async_remote_copy(
        src_ref=src,
        dst_ref=dst,
        send_sem=send,
        recv_sem=recv,
        device_id={axis: peer},
        device_id_type=MESH,
    )


def each(lo, hi, fn):
    def body(s, c):
        fn(s)
        return c

    lax.fori_loop(lo, hi, body, 0)


def rows_of(p):
    return pl.ds(pl.multiple_of(p * BODY, BODY), BODY)


def exchange_start(src, dst, send, recv, own, me):
    def go(o):
        p = expert_peer(me, o)
        remote(
            src.at[rows_of(p), :], dst.at[rows_of(me), :], send.at[p], recv.at[me], "expert", p
        ).start()

    for o in FAR_FIRST:
        go(o)
    pltpu.make_async_copy(src.at[rows_of(me), :], dst.at[rows_of(me), :], own).start()


def exchange_wait(src, dst, send, recv, own, me):
    pltpu.make_async_copy(src.at[rows_of(me), :], dst.at[rows_of(me), :], own).wait()

    def go(o):
        p = expert_peer(me, o)
        remote(
            src.at[rows_of(p), :], dst.at[rows_of(p), :], send.at[p], recv.at[p], "expert", p
        ).wait_recv()

    each(1, PEERS, go)


def exchange_sent(src, dst, send, recv, me):
    def go(o):
        p = expert_peer(me, o)
        remote(
            src.at[rows_of(p), :], dst.at[rows_of(p), :], send.at[p], recv.at[p], "expert", p
        ).wait_send()

    each(1, PEERS, go)


def pack(dst, body_hot, rest_hot, src):
    rest = None
    for q in range(4):
        part = src[:, q * QUARTER : (q + 1) * QUARTER]
        dst[:, q * QUARTER : (q + 1) * QUARTER] = dot(body_hot[...], part).astype(bf16)
        more = dot(rest_hot[q], part)
        rest = more if rest is None else rest + more
    dst[:, D:BLOCK] = rest.astype(bf16)


def pack_half(dst, body_hot, rest_hot, src):
    for q in range(2):
        d = slice(q * QUARTER, (q + 1) * QUARTER)
        dst[:, d] = dot(body_hot[...], src[:, d]).astype(bf16)
    rest = None
    for q in range(4):
        more = dot(rest_hot[q], src[:, q * PIECE : (q + 1) * PIECE])
        rest = more if rest is None else rest + more
    dst[:, HALF:HALF_BLOCK] = rest.astype(bf16)


def rest_pick(q):
    i, j = iota((64, 256), 0), iota((64, 256), 1)
    return one_hot(j == (i // REST) * BODY + q * REST + lax.rem(i, REST))


def rest_put(q):
    j, i = iota((256, 64), 0), iota((256, 64), 1)
    return one_hot(j == (i // REST) * BODY + q * REST + lax.rem(i, REST))


def unpack(dst, src):
    dst[0:256, :] = src[:, 0:D]
    for q in range(4):
        dst[256:ROWS, q * QUARTER : (q + 1) * QUARTER] = dot(rest_pick(q), src[:, D:BLOCK]).astype(
            bf16
        )
    dst[ROWS:PADDED, :] = jnp.zeros((PADDED - ROWS, D), bf16)


def turned_row(ref, k):
    return jnp.transpose(jnp.broadcast_to(ref[k : k + 1, :].astype(f32), (TOK, TOK)))


def unpack_half(dst, src, phase):
    lo = phase * HALF
    dst[0:256, lo : lo + HALF] = src[:, 0:HALF]
    for q in range(4):
        at = lo + q * PIECE
        dst[256:ROWS, at : at + PIECE] = dot(rest_pick(q), src[:, HALF:HALF_BLOCK]).astype(bf16)
    dst[ROWS:PADDED, lo : lo + HALF] = jnp.zeros((PADDED - ROWS, HALF), bf16)


def three_parts(v):
    high = v.astype(bf16)
    low = v - high.astype(f32)
    middle = low.astype(bf16)
    return high.astype(f32), middle.astype(f32), low - middle.astype(f32)


def route_hots(routes, body_t, rest_t, body_k, rest_k):
    lane, row = iota((TOK, TOK), 1), iota((TOK, TOK), 0)
    r = [turned_row(routes, k) for k in range(2)]
    hit = [lane.astype(f32) == r[k] for k in range(2)]
    hits = one_hot(jnp.logical_or(hit[0], hit[1]))
    rank = dot(one_hot(lane < row), hits)
    for k in range(2):
        mine = jnp.sum(jnp.where(hit[k], rank, 0.0), axis=1, keepdims=True)
        base = r[k][:, 0:1] * BODY + mine
        at_body = jnp.where(mine < BODY, base, -1.0)
        at_rest = jnp.where(mine < BODY, -1000.0, base - BODY)
        wide_body = jnp.broadcast_to(at_body, (TOK, TOK))
        wide_rest = jnp.broadcast_to(at_rest, (TOK, TOK))
        slot = iota((TOK, 256), 1).astype(f32)
        body_k[k] = one_hot(slot == jnp.broadcast_to(at_body, (TOK, 256)))
        for q in range(4):
            rest_k[k, q] = one_hot(slot == jnp.broadcast_to(at_rest, (TOK, 256)) + REST * q)
        turned_body, turned_rest = jnp.transpose(wide_body), jnp.transpose(wide_rest)
        for half in range(2):
            rows = slice(half * TOK, (half + 1) * TOK)
            here = (row + half * TOK).astype(f32)
            body_t[rows, k * TOK : (k + 1) * TOK] = one_hot(here == turned_body)
            for q in range(4):
                rest_t[q, rows, k * TOK : (k + 1) * TOK] = one_hot(here == turned_rest + REST * q)


def attend_frame(i, core, qs, ks, vs, out):
    scale = HD**-0.5
    q = qs[i]
    near = dot_nt(q, ks[i].reshape(2 * TOK, HD))
    near = jnp.where(iota((TOK, 2 * TOK), 1) // TOK <= core, near, -1e30)
    top = jnp.max(near, axis=1, keepdims=True)
    if i:
        far = dot_nt(q, ks[0:i].reshape(2 * i * TOK, HD))
        top = jnp.maximum(top, jnp.max(far, axis=1, keepdims=True))
    near = jnp.exp((near - top) * scale)
    total = jnp.sum(near, axis=1, keepdims=True)
    acc = dot(near.astype(bf16), vs[i].reshape(2 * TOK, HD))
    if i:
        far = jnp.exp((far - top) * scale)
        total = total + jnp.sum(far, axis=1, keepdims=True)
        acc = acc + dot(far.astype(bf16), vs[0:i].reshape(2 * i * TOK, HD))
    out[i] = (acc / total).astype(bf16)


def layer_kernel(
    tok_any,
    cot_any,
    action_any,
    table_any,
    gain_any,
    routes_any,
    gates_any,
    predicted_any,
    q_any,
    k_any,
    v_any,
    up_any,
    down_any,
    layer_any,
    stream_grad_any,
    up_grad_any,
    down_grad_any,
    tok,
    cot,
    action,
    table,
    gain,
    routes,
    gates,
    predicted,
    layer_out,
    stream_grad,
    up_grad,
    down_grad,
    up_w,
    down_w,
    qs,
    ks,
    vs,
    heads_out,
    attended,
    stream,
    rows,
    body_t,
    rest_t,
    body_k,
    rest_k,
    grad_send,
    grad_in,
    first_send,
    first_in,
    second_send,
    second_in,
    squares,
    inv_slots,
    pre,
    out_send,
    out_in,
    back_send,
    back_in,
    xs,
    gs,
    turned,
    act,
    act_t,
    grad_act,
    grad_pre,
    grad_norm,
    scaled_back,
    down_part,
    up_part,
    down_pair,
    up_pair,
    down_right,
    down_left,
    up_right,
    up_left,
    fetch_sem,
    result_sem,
    w_sem,
    own_sem,
    qkv_own,
    qkv_send,
    qkv_recv,
    hand_send,
    hand_recv,
    o_own,
    o_send,
    o_recv,
    x_send,
    x_recv,
    pair_send,
    pair_recv,
    ring_send,
    ring_recv,
):
    tm, ex = lax.axis_index("tm"), lax.axis_index("expert")
    chip, core = tm // 2, lax.rem(tm, 2)
    sibling = tm + 1 - 2 * core
    right, left = lax.rem(tm + 2, PEERS), lax.rem(tm + PEERS - 2, PEERS)

    def fetch(n, src, dst):
        return pltpu.make_async_copy(src, dst, fetch_sem.at[n])

    first = [
        fetch(0, routes_any, routes),
        fetch(1, gates_any, gates),
        fetch(2, predicted_any, predicted),
        fetch(3, cot_any, cot),
    ]
    later = [
        fetch(4, tok_any, tok),
        fetch(5, action_any, action),
        fetch(6, table_any, table),
        fetch(7, gain_any, gain),
    ]
    up_load = pltpu.make_async_copy(up_any, up_w, w_sem.at[0])
    down_load = pltpu.make_async_copy(down_any, down_w, w_sem.at[1])

    def columns(p):
        return pl.ds(pl.multiple_of(p * HD, HD), HD)

    def head_of(phase, t):
        return columns(phase * CHIPS + t)

    def device_of(t):
        return 2 * t + core

    def other_chip(o):
        return lax.rem(chip + o, CHIPS)

    def far_chip(s):
        half = s // 2
        return other_chip(4 + half - 2 * half * lax.rem(s, 2))

    def head_copy(n, phase, t, slot):
        src = (q_any, k_any, v_any)[n].at[:, head_of(phase, t)]
        dst = qs.at[phase, slot] if n == 0 else (ks, vs)[n - 1].at[phase, slot, core]
        return src, dst

    def head_remote(n, phase, t, slot):
        src, dst = head_copy(n, phase, t, slot)
        return remote(
            src, dst, qkv_send.at[phase, n, t], qkv_recv.at[phase, n, slot], "tm", device_of(t)
        )

    own_heads = [
        pltpu.make_async_copy(*head_copy(n, phase, chip, chip), qkv_own.at[phase, n])
        for phase in range(PHASES)
        for n in range(3)
    ]

    barrier = pltpu.get_barrier_semaphore()

    def greet(o):
        pl.semaphore_signal(
            barrier, inc=1, device_id={"tm": tm_peer(tm, o)}, device_id_type=MESH
        )
        pl.semaphore_signal(
            barrier, inc=1, device_id={"expert": expert_peer(ex, o)}, device_id_type=MESH
        )

    each(1, PEERS, greet)
    for copy in first + own_heads + later + [down_load, up_load]:
        copy.start()

    for copy in first:
        copy.wait()
    route_hots(routes, body_t, rest_t, body_k, rest_k)
    kept = turned_row(predicted, 0)[:, 0:1]
    gate = [turned_row(gates, k)[:, 0:1] for k in range(2)]
    upstream = cot[...].astype(f32) * kept
    for k in range(2):
        rows[k * TOK : (k + 1) * TOK, :] = (gate[k] * upstream).astype(bf16)
    pack(grad_send, body_t, rest_t, rows)

    pl.semaphore_wait(barrier, 2 * (PEERS - 1))

    def send_keys(phase):
        def go(s):
            t = far_chip(s)
            head_remote(1, phase, t, chip).start()
            head_remote(2, phase, t, chip).start()

        each(1, CHIPS, go)

    def send_queries(phase):
        each(1, CHIPS, lambda s: head_remote(0, phase, far_chip(s), chip).start())

    send_keys(0)
    send_queries(0)
    exchange_start(grad_send, grad_in, x_send.at[0], x_recv.at[0], own_sem.at[0], ex)
    send_keys(1)

    for copy in own_heads:
        copy.wait()

    def hand(phase, n, which):
        ref = (ks, vs)[n].at[phase, :, which]
        return remote(ref, ref, hand_send.at[phase, n], hand_recv.at[phase, n], "tm", sibling)

    def wait_keys(phase):
        def go(o):
            t = other_chip(o)
            head_remote(1, phase, t, t).wait_recv()
            head_remote(2, phase, t, t).wait_recv()

        each(1, CHIPS, go)
        for n in range(2):
            hand(phase, n, core).start()

    def wait_handed(phase):
        for n in range(2):
            hand(phase, n, 1 - core).wait_recv()

    def head_out(phase, t, slot):
        return remote(
            heads_out.at[phase, t],
            attended.at[:, head_of(phase, slot)],
            o_send.at[phase, t],
            o_recv.at[phase, slot],
            "tm",
            device_of(t),
        )

    def own_out(phase):
        return pltpu.make_async_copy(
            heads_out.at[phase, chip], attended.at[:, head_of(phase, chip)], o_own.at[phase]
        )

    def attend(phase):
        def go(s):
            half = (s + 1) // 2
            i = lax.rem(chip + 4 + half - 2 * half * lax.rem(s, 2), CHIPS)

            @pl.when(i != chip)
            def _():
                head_remote(0, phase, i, i).wait_recv()

            lax.switch(
                i,
                [
                    functools.partial(
                        attend_frame,
                        n,
                        core,
                        qs.at[phase],
                        ks.at[phase],
                        vs.at[phase],
                        heads_out.at[phase],
                    )
                    for n in range(CHIPS)
                ],
            )

            @pl.when(i != chip)
            def _():
                head_out(phase, i, chip).start()

        each(0, CHIPS, go)
        own_out(phase).start()

    def wait_attended(phase):
        own_out(phase).wait()

        def go(o):
            t = other_chip(o)
            head_out(phase, t, t).wait_recv()

        each(1, CHIPS, go)

    def columns_done(phase):
        d = slice(phase * HALF, (phase + 1) * HALF)
        total = tok[:, d].astype(f32) + attended[:, d].astype(f32) + action_row[:, d]
        stream[:, d] = total.astype(bf16)
        held = stream[:, d].astype(f32)
        part = (held * gain[:, d]).astype(bf16)
        rows[0:TOK, 0:HALF] = part
        rows[TOK : 2 * TOK, 0:HALF] = part
        return jnp.sum(held * held, axis=1, keepdims=True)

    def turn(phase):
        for n in range(4):
            lo = phase * HALF + n * 256
            turned[phase * 4 + n] = jnp.transpose(xs[:, lo : lo + 256]).reshape(2, 128, PADDED)

    wait_keys(0)
    wait_handed(0)
    attend(0)
    send_queries(1)

    down_load.wait()
    exchange_wait(grad_send, grad_in, x_send.at[0], x_recv.at[0], own_sem.at[0], ex)
    unpack(gs, grad_in)

    def act_back(n):
        f = pl.ds(pl.multiple_of(n * 256, 256), 256)
        grad_act[:, f] = dot_nt(gs[0:ROWS, :], down_w[f, :])

    each(0, FF // 256, act_back)
    for copy in later:
        copy.wait()
    choose = one_hot(iota((8, ACTIONS), 1) == jnp.broadcast_to(action[...], (8, ACTIONS)))
    action_row = dot(choose, table[...])[0:1, :]

    wait_keys(1)
    wait_attended(0)
    squares[...] = columns_done(0)
    pack_half(first_send, body_t, rest_t, rows)
    exchange_start(first_send, first_in, x_send.at[1], x_recv.at[1], own_sem.at[1], ex)
    wait_handed(1)
    attend(1)
    wait_attended(1)

    inv_rms = lax.rsqrt((squares[...] + columns_done(1)) * (1.0 / D) + norm_eps)
    pack_half(second_send, body_t, rest_t, rows)
    lane = iota((TOK, TOK), 1)
    in_body = in_rest = jnp.zeros((TOK, TOK), f32)
    for n, part in enumerate(three_parts(inv_rms)):
        in_body = jnp.where(lane == n, part, in_body)
        in_rest = jnp.where(lane == n + 3, part, in_rest)
    in_body, in_rest = in_body.astype(bf16), in_rest.astype(bf16)
    second_send[:, HALF_BLOCK:] = (
        dot(body_t[:, 0:TOK] + body_t[:, TOK:], in_body)
        + dot(rest_t[0, :, 0:TOK] + rest_t[0, :, TOK:], in_rest)
    ).astype(bf16)
    exchange_start(second_send, second_in, x_send.at[4], x_recv.at[4], own_sem.at[4], ex)

    up_load.wait()
    exchange_wait(first_send, first_in, x_send.at[1], x_recv.at[1], own_sem.at[1], ex)
    unpack_half(xs, first_in, 0)

    def first_up(n):
        f = pl.ds(pl.multiple_of(n * 256, 256), 256)
        pre[:, f] = dot(xs[0:ROWS, 0:HALF], up_w[0:HALF, f])

    each(0, FF // 256, first_up)
    turn(0)
    exchange_wait(second_send, second_in, x_send.at[4], x_recv.at[4], own_sem.at[4], ex)
    unpack_half(xs, second_in, 1)
    parts = second_in[:, HALF_BLOCK:]
    lane = iota((256, TOK), 1)
    inv_slots[0:256, :] = jnp.sum(
        jnp.where(lane < 3, parts.astype(f32), 0.0), axis=1, keepdims=True
    )
    lane = iota((64, TOK), 1)
    inv_slots[256:ROWS, :] = jnp.sum(
        jnp.where(jnp.logical_and(lane >= 3, lane < 6), dot(rest_pick(0), parts), 0.0),
        axis=1,
        keepdims=True,
    )

    act[ROWS:PADDED, :] = jnp.zeros((PADDED - ROWS, FF), bf16)
    grad_pre[ROWS:PADDED, :] = jnp.zeros((PADDED - ROWS, FF), bf16)

    grad_norm[ROWS:PADDED, :] = jnp.zeros((PADDED - ROWS, FF), bf16)

    def expert_up(n):
        f = pl.ds(pl.multiple_of(n * 256, 256), 256)
        inv = inv_slots[...]
        v = (pre[:, f] + dot(xs[0:ROWS, HALF:D], up_w[HALF:D, f])) * inv
        th = jnp.tanh(gelu_coef * (v + 0.044715 * v * v * v))
        act[0:ROWS, f] = (0.5 * v * (1.0 + th)).astype(bf16)
        slope = 0.5 * (1.0 + th) + 0.5 * v * (1.0 - th * th) * gelu_coef * (
            1.0 + 3.0 * 0.044715 * v * v
        )
        back = grad_act[:, f] * slope
        grad_pre[0:ROWS, f] = back.astype(bf16)
        grad_norm[0:ROWS, f] = (back * inv).astype(bf16)
        act_t[pl.ds(n * 2, 2)] = jnp.transpose(act[:, f]).reshape(2, 2, 64, PADDED)

    each(0, FF // 256, expert_up)

    def down_weights(which):
        def go(n):
            d = pl.ds(pl.multiple_of(n * 512, 512), 512)
            part = dot(act_t[:, which].reshape(CHIPS * 64, PADDED), gs[:, d]).astype(bf16)
            down_part[:, which, :, d] = part.reshape(CHIPS, 64, 512)

        each(0, D // 512, go)

    def up_weights(which):
        def go(n):
            part = dot(turned[pl.ds(n * 2, 2), which].reshape(256, PADDED), grad_norm[...])
            up_part[pl.ds(n * 2, 2), which] = part.astype(bf16).reshape(2, 128, FF)

        each(0, CHIPS // 2, go)

    def pair(n, t):
        part, got = ((down_part, down_pair), (up_part, up_pair))[n]
        return remote(
            part.at[t, 1 - core], got.at[t], pair_send.at[n, t], pair_recv.at[n, t], "tm", sibling
        )

    def pair_start(n):
        for o in (7, 1, 6, 2, 5, 3, 4, 0):
            pair(n, other_chip(o)).start()

    def pair_wait(n, offsets):
        for o in offsets:
            pair(n, other_chip(o)).wait_recv()

    near_chips, far_chips = (7, 1), (6, 2, 5, 3, 4, 0)

    down_weights(1 - core)
    pair_start(0)
    turn(1)
    down_weights(core)
    up_weights(1 - core)
    pair_start(1)

    def send_rows(dst, product):
        rest = None
        for q in range(4):
            part = product(q).astype(bf16)
            dst[:, q * QUARTER : (q + 1) * QUARTER] = part[0:256, :]
            more = dot(rest_put(q), part[256:ROWS, :])
            rest = more if rest is None else rest + more
        dst[:, D:BLOCK] = rest.astype(bf16)

    streams = (
        (down_pair, down_part, down_right, 0, 32, 1, right),
        (down_pair, down_part, down_left, 32, 32, -1, left),
        (up_pair, up_part, up_right, 0, 64, 1, right),
        (up_pair, up_part, up_left, 64, 64, -1, left),
    )

    def chip_sum(n, t):
        pair, part, _, lo, size, _, _ = streams[n]
        return (
            pair[t, lo : lo + size, :].astype(f32) + part[t, core, lo : lo + size, :].astype(f32)
        )

    def hop(n, src, s):
        _, _, slots, _, _, _, to = streams[n]
        return remote(src, slots.at[s], ring_send.at[n, s], ring_recv.at[n, s], "tm", to)

    def first_hop(n):
        pair, _, _, lo, size, way, _ = streams[n]
        t = lax.rem(chip - way + CHIPS, CHIPS)
        pair[t, lo : lo + size, :] = chip_sum(n, t).astype(bf16)
        hop(n, pair.at[t, lo : lo + size, :], 0).start()

    def next_hop(n, s):
        _, _, slots, _, _, way, _ = streams[n]
        t = lax.rem(chip - way * (1 + s) + 2 * CHIPS, CHIPS)
        hop(n, slots.at[s - 1], s - 1).wait_recv()
        slots[s - 1] = (slots[s - 1].astype(f32) + chip_sum(n, t)).astype(bf16)
        hop(n, slots.at[s - 1], s).start()

    pair_wait(0, near_chips)
    first_hop(0)
    first_hop(1)
    up_weights(core)
    pair_wait(1, near_chips)
    first_hop(2)
    first_hop(3)
    send_rows(
        out_send, lambda q: dot(act[0:ROWS, :], down_w[:, q * QUARTER : (q + 1) * QUARTER])
    )
    exchange_start(out_send, out_in, x_send.at[2], x_recv.at[2], own_sem.at[2], ex)

    pair_wait(0, far_chips)
    pair_wait(1, far_chips)
    next_hop(0, 1)
    next_hop(1, 1)

    send_rows(
        back_send, lambda q: dot_nt(grad_pre[0:ROWS, :], up_w[q * QUARTER : (q + 1) * QUARTER, :])
    )
    exchange_start(back_send, back_in, x_send.at[3], x_recv.at[3], own_sem.at[3], ex)

    def hops(s):
        next_hop(2, s)
        next_hop(3, s)
        next_hop(0, s + 1)
        next_hop(1, s + 1)

    each(1, CHIPS - 2, hops)
    next_hop(2, CHIPS - 2)
    next_hop(3, CHIPS - 2)

    exchange_wait(out_send, out_in, x_send.at[2], x_recv.at[2], own_sem.at[2], ex)
    for q in range(4):
        d = slice(q * QUARTER, (q + 1) * QUARTER)
        mixed = stream[:, d].astype(f32)
        for k in range(2):
            picked = dot(body_k[k], out_in[:, d]) + dot(rest_k[k, q], out_in[:, D:BLOCK])
            mixed = mixed + gate[k] * picked
        layer_out[:, d] = mixed.astype(bf16)
    layer_store = pltpu.make_async_copy(layer_out, layer_any, result_sem.at[0])
    layer_store.start()

    exchange_wait(back_send, back_in, x_send.at[3], x_recv.at[3], own_sem.at[3], ex)
    held = stream[...].astype(f32)
    inv_rms = lax.rsqrt(jnp.mean(held * held, axis=1, keepdims=True) + norm_eps)
    both = jnp.zeros((TOK, 1), f32)
    for q in range(4):
        d = slice(q * QUARTER, (q + 1) * QUARTER)
        back = dot(body_k[0] + body_k[1], back_in[:, d]) + dot(
            rest_k[0, q] + rest_k[1, q], back_in[:, D:BLOCK]
        )
        back = back * gain[:, d]
        scaled_back[:, d] = back
        unit = stream[:, d].astype(f32) * inv_rms
        both = both + jnp.sum(back * unit, axis=1, keepdims=True)
    both = both * (1.0 / D)
    for q in range(4):
        d = slice(q * QUARTER, (q + 1) * QUARTER)
        unit = stream[:, d].astype(f32) * inv_rms
        up_here = cot[:, d].astype(f32) * kept
        stream_grad[:, d] = (up_here + inv_rms * (scaled_back[:, d] - unit * both)).astype(bf16)

    stream_store = pltpu.make_async_copy(stream_grad, stream_grad_any, result_sem.at[1])
    stream_store.start()

    def sent(o):
        t = other_chip(o)
        for phase in range(PHASES):
            for n in range(3):
                head_remote(n, phase, t, t).wait_send()
            head_out(phase, t, t).wait_send()

    each(1, CHIPS, sent)
    for phase in range(PHASES):
        for n in range(2):
            hand(phase, n, core).wait_send()
    for n, (a, b) in enumerate(
        (
            (grad_send, grad_in),
            (first_send, first_in),
            (out_send, out_in),
            (back_send, back_in),
            (second_send, second_in),
        )
    ):
        exchange_sent(a, b, x_send.at[n], x_recv.at[n], ex)

    def pairs_sent(t):
        pair(0, t).wait_send()
        pair(1, t).wait_send()

    each(0, CHIPS, pairs_sent)

    for n, out in ((0, down_grad), (1, down_grad), (2, up_grad), (3, up_grad)):
        _, _, slots, lo, size, _, _ = streams[n]
        hop(n, slots.at[CHIPS - 2], CHIPS - 2).wait_recv()
        out[lo : lo + size, :] = (slots[CHIPS - 2].astype(f32) + chip_sum(n, chip)).astype(bf16)

    up_store = pltpu.make_async_copy(up_grad, up_grad_any, result_sem.at[2])
    down_store = pltpu.make_async_copy(down_grad, down_grad_any, result_sem.at[3])
    up_store.start()
    down_store.start()

    def hops_sent(s):
        for n, (_, _, slots, _, _, _, _) in enumerate(streams):
            hop(n, slots.at[s], s).wait_send()

    each(0, CHIPS - 1, hops_sent)
    for copy in (layer_store, stream_store, up_store, down_store):
        copy.wait()


def deliver_kernel(*refs):
    made, given, held, came, left = refs[0:4], refs[4:8], refs[8:12], refs[12], refs[13]
    inward = [pltpu.make_async_copy(made[n], held[n], came.at[n]) for n in range(4)]
    outward = [pltpu.make_async_copy(held[n], given[n], left.at[n]) for n in range(4)]
    for copy in inward:
        copy.start()
    for n in range(4):
        inward[n].wait()
        outward[n].start()
    for copy in outward:
        copy.wait()


def local(
    tokens,
    queries,
    key_rows,
    values,
    actions,
    action_table,
    norm_gain,
    routes,
    gate_probs,
    predicted,
    cotangent,
    up_weight,
    down_weight,
):
    hbm = pl.BlockSpec(memory_space=pl.ANY)
    dma = pltpu.SemaphoreType.DMA
    block = pltpu.VMEM((256, BLOCK), bf16)
    results = (
        jax.ShapeDtypeStruct((TOK, D), bf16),
        jax.ShapeDtypeStruct((TOK, D), bf16),
        jax.ShapeDtypeStruct((D // PEERS, FF), bf16),
        jax.ShapeDtypeStruct((FF // PEERS, D), bf16),
    )
    made = pl.pallas_call(
        layer_kernel,
        out_shape=results,
        in_specs=[hbm] * 13,
        out_specs=(hbm,) * 4,
        scratch_shapes=[
            pltpu.VMEM((TOK, D), bf16),
            pltpu.VMEM((TOK, D), bf16),
            pltpu.VMEM((1, 1), jnp.int32),
            pltpu.VMEM((ACTIONS, D), bf16),
            pltpu.VMEM((1, D), f32),
            pltpu.VMEM((2, TOK), jnp.int32),
            pltpu.VMEM((2, TOK), f32),
            pltpu.VMEM((1, TOK), jnp.int32),
            pltpu.VMEM((TOK, D), bf16),
            pltpu.VMEM((TOK, D), bf16),
            pltpu.VMEM((D // PEERS, FF), bf16),
            pltpu.VMEM((FF // PEERS, D), bf16),
            pltpu.VMEM((D, FF), bf16),
            pltpu.VMEM((FF, D), bf16),
            pltpu.VMEM((PHASES, CHIPS, TOK, HD), bf16),
            pltpu.VMEM((PHASES, CHIPS, 2, TOK, HD), bf16),
            pltpu.VMEM((PHASES, CHIPS, 2, TOK, HD), bf16),
            pltpu.VMEM((PHASES, CHIPS, TOK, HD), bf16),
            pltpu.VMEM((TOK, D), bf16),
            pltpu.VMEM((TOK, D), bf16),
            pltpu.VMEM((2 * TOK, D), bf16),
            pltpu.VMEM((256, 256), bf16),
            pltpu.VMEM((4, 256, 256), bf16),
            pltpu.VMEM((2, TOK, 256), bf16),
            pltpu.VMEM((2, 4, TOK, 256), bf16),
        ]
        + [block] * 2
        + [
            pltpu.VMEM((256, HALF_BLOCK), bf16),
            pltpu.VMEM((256, HALF_BLOCK), bf16),
            pltpu.VMEM((256, HALF_BLOCK + TOK), bf16),
            pltpu.VMEM((256, HALF_BLOCK + TOK), bf16),
            pltpu.VMEM((TOK, 1), f32),
            pltpu.VMEM((ROWS, 1), f32),
            pltpu.VMEM((ROWS, FF), f32),
        ]
        + [block] * 4
        + [
            pltpu.VMEM((PADDED, D), bf16),
            pltpu.VMEM((PADDED, D), bf16),
            pltpu.VMEM((CHIPS, 2, 128, PADDED), bf16),
            pltpu.VMEM((PADDED, FF), bf16),
            pltpu.VMEM((CHIPS, 2, 64, PADDED), bf16),
            pltpu.VMEM((ROWS, FF), f32),
            pltpu.VMEM((PADDED, FF), bf16),
            pltpu.VMEM((PADDED, FF), bf16),
            pltpu.VMEM((TOK, D), f32),
            pltpu.VMEM((CHIPS, 2, 64, D), bf16),
            pltpu.VMEM((CHIPS, 2, 128, FF), bf16),
            pltpu.VMEM((CHIPS, 64, D), bf16),
            pltpu.VMEM((CHIPS, 128, FF), bf16),
            pltpu.VMEM((CHIPS - 1, 32, D), bf16),
            pltpu.VMEM((CHIPS - 1, 32, D), bf16),
            pltpu.VMEM((CHIPS - 1, 64, FF), bf16),
            pltpu.VMEM((CHIPS - 1, 64, FF), bf16),
            dma((8,)),
            dma((4,)),
            dma((2,)),
            dma((5,)),
            dma((PHASES, 3)),
            dma((PHASES, 3, CHIPS)),
            dma((PHASES, 3, CHIPS)),
            dma((PHASES, 2)),
            dma((PHASES, 2)),
            dma((PHASES,)),
            dma((PHASES, CHIPS)),
            dma((PHASES, CHIPS)),
            dma((5, PEERS)),
            dma((5, PEERS)),
            dma((2, CHIPS)),
            dma((2, CHIPS)),
            dma((4, CHIPS - 1)),
            dma((4, CHIPS - 1)),
        ],
        compiler_params=pltpu.CompilerParams(
            collective_id=0, has_side_effects=True, vmem_limit_bytes=62 * 2**20
        ),
        name="layer",
    )(
        tokens.reshape(TOK, D),
        cotangent.reshape(TOK, D),
        actions,
        action_table,
        norm_gain.reshape(1, D),
        routes.reshape(TOK, 2).T,
        gate_probs.reshape(TOK, 2).T,
        predicted.reshape(1, TOK),
        queries.reshape(TOK, D),
        key_rows.reshape(TOK, D),
        values.reshape(TOK, D),
        up_weight.reshape(D, FF),
        down_weight.reshape(FF, D),
    )
    layer_out, stream_grad, up_grad, down_grad = pl.pallas_call(
        deliver_kernel,
        out_shape=results,
        in_specs=[hbm] * 4,
        out_specs=(hbm,) * 4,
        scratch_shapes=[pltpu.VMEM(r.shape, r.dtype) for r in results] + [dma((4,)), dma((4,))],
        name="deliver",
    )(*made)
    return (
        layer_out.reshape(tokens.shape),
        stream_grad.reshape(tokens.shape),
        up_grad.reshape(1, D // PEERS, FF),
        down_grad.reshape(1, FF // PEERS, D),
    )


def solution(mesh):
    rows = P("expert", "tm", None, None)
    in_specs = (
        rows,
        rows,
        rows,
        rows,
        P("expert", "tm"),
        P(),
        P(),
        rows,
        rows,
        P("expert", "tm", None),
        rows,
        P("expert", None, None),
        P("expert", None, None),
    )
    out_specs = (rows, rows, P("expert", "tm", None), P("expert", "tm", None))
    return jax.shard_map(local, mesh=mesh, in_specs=in_specs, out_specs=out_specs, check_vma=False)
```

```python
import functools

import jax
import jax.numpy as jnp
from jax import lax
from jax.experimental import pallas as pl
from jax.experimental.pallas import tpu as pltpu
from jax.sharding import PartitionSpec as P

MESH = pl.DeviceIdType.MESH
PEERS = 16
HEADS = 16
HD = 128
D = 2048
FF = 1024
ACTIONS = 64
TOK = 128
CHIPS = 8
BODY = 16
REST = 4
ROWS = 320
PADDED = 384
QUARTER = 512
BLOCK = D + QUARTER
HALF = D // 2
PIECE = HALF // 4
HALF_BLOCK = HALF + PIECE
PHASES = 2

norm_eps = 1e-06
gelu_coef = 0.7978845608028654

f32 = jnp.float32
bf16 = jnp.bfloat16


def dot(a, b):
    return jnp.dot(a, b, preferred_element_type=f32)


def dot_nt(a, b):
    return lax.dot_general(a, b, (((1,), (1,)), ((), ())), preferred_element_type=f32)


def iota(shape, dim):
    return lax.broadcasted_iota(jnp.int32, shape, dim)


def one_hot(mask):
    return mask.astype(f32).astype(bf16)


def tm_peer(me, o):
    return lax.rem(me + o, PEERS)


def expert_peer(me, o):
    y, x = me // 4, lax.rem(me, 4)
    return lax.rem(y + o // 4, 4) * 4 + lax.rem(x + lax.rem(o, 4), 4)


FAR_FIRST = (10, 2, 8, 6, 14, 9, 11, 5, 7, 13, 15, 1, 3, 4, 12)


def far_first(s):
    half = s // 2
    return 8 + half - 2 * half * lax.rem(s, 2)


def remote(src, dst, send, recv, axis, peer):
    return pltpu.make_async_remote_copy(
        src_ref=src,
        dst_ref=dst,
        send_sem=send,
        recv_sem=recv,
        device_id={axis: peer},
        device_id_type=MESH,
    )


def each(lo, hi, fn):
    def body(s, c):
        fn(s)
        return c

    lax.fori_loop(lo, hi, body, 0)


def rows_of(p):
    return pl.ds(pl.multiple_of(p * BODY, BODY), BODY)


def exchange_start(src, dst, send, recv, own, me):
    def go(o):
        p = expert_peer(me, o)
        remote(
            src.at[rows_of(p), :], dst.at[rows_of(me), :], send.at[p], recv.at[me], "expert", p
        ).start()

    for o in FAR_FIRST:
        go(o)
    pltpu.make_async_copy(src.at[rows_of(me), :], dst.at[rows_of(me), :], own).start()


def exchange_wait(src, dst, send, recv, own, me):
    pltpu.make_async_copy(src.at[rows_of(me), :], dst.at[rows_of(me), :], own).wait()

    def go(o):
        p = expert_peer(me, o)
        remote(
            src.at[rows_of(p), :], dst.at[rows_of(p), :], send.at[p], recv.at[p], "expert", p
        ).wait_recv()

    each(1, PEERS, go)


def exchange_sent(src, dst, send, recv, me):
    def go(o):
        p = expert_peer(me, o)
        remote(
            src.at[rows_of(p), :], dst.at[rows_of(p), :], send.at[p], recv.at[p], "expert", p
        ).wait_send()

    each(1, PEERS, go)


def pack(dst, body_hot, rest_hot, src):
    rest = None
    for q in range(4):
        part = src[:, q * QUARTER : (q + 1) * QUARTER]
        dst[:, q * QUARTER : (q + 1) * QUARTER] = dot(body_hot[...], part).astype(bf16)
        more = dot(rest_hot[q], part)
        rest = more if rest is None else rest + more
    dst[:, D:BLOCK] = rest.astype(bf16)


def pack_half(dst, body_hot, rest_hot, src):
    for q in range(2):
        d = slice(q * QUARTER, (q + 1) * QUARTER)
        dst[:, d] = dot(body_hot[...], src[:, d]).astype(bf16)
    rest = None
    for q in range(4):
        more = dot(rest_hot[q], src[:, q * PIECE : (q + 1) * PIECE])
        rest = more if rest is None else rest + more
    dst[:, HALF:HALF_BLOCK] = rest.astype(bf16)


def rest_pick(q):
    i, j = iota((64, 256), 0), iota((64, 256), 1)
    return one_hot(j == (i // REST) * BODY + q * REST + lax.rem(i, REST))


def rest_put(q):
    j, i = iota((256, 64), 0), iota((256, 64), 1)
    return one_hot(j == (i // REST) * BODY + q * REST + lax.rem(i, REST))


def unpack(dst, src):
    dst[0:256, :] = src[:, 0:D]
    for q in range(4):
        dst[256:ROWS, q * QUARTER : (q + 1) * QUARTER] = dot(rest_pick(q), src[:, D:BLOCK]).astype(
            bf16
        )
    dst[ROWS:PADDED, :] = jnp.zeros((PADDED - ROWS, D), bf16)


def turned_row(ref, k):
    return jnp.transpose(jnp.broadcast_to(ref[k : k + 1, :].astype(f32), (TOK, TOK)))


def unpack_half(dst, src, phase):
    lo = phase * HALF
    dst[0:256, lo : lo + HALF] = src[:, 0:HALF]
    for q in range(4):
        at = lo + q * PIECE
        dst[256:ROWS, at : at + PIECE] = dot(rest_pick(q), src[:, HALF:HALF_BLOCK]).astype(bf16)
    dst[ROWS:PADDED, lo : lo + HALF] = jnp.zeros((PADDED - ROWS, HALF), bf16)


def three_parts(v):
    high = v.astype(bf16)
    low = v - high.astype(f32)
    middle = low.astype(bf16)
    return high.astype(f32), middle.astype(f32), low - middle.astype(f32)


def route_hots(routes, body_t, rest_t, body_k, rest_k):
    lane, row = iota((TOK, TOK), 1), iota((TOK, TOK), 0)
    r = [turned_row(routes, k) for k in range(2)]
    hit = [lane.astype(f32) == r[k] for k in range(2)]
    hits = one_hot(jnp.logical_or(hit[0], hit[1]))
    rank = dot(one_hot(lane < row), hits)
    for k in range(2):
        mine = jnp.sum(jnp.where(hit[k], rank, 0.0), axis=1, keepdims=True)
        base = r[k][:, 0:1] * BODY + mine
        at_body = jnp.where(mine < BODY, base, -1.0)
        at_rest = jnp.where(mine < BODY, -1000.0, base - BODY)
        wide_body = jnp.broadcast_to(at_body, (TOK, TOK))
        wide_rest = jnp.broadcast_to(at_rest, (TOK, TOK))
        slot = iota((TOK, 256), 1).astype(f32)
        body_k[k] = one_hot(slot == jnp.broadcast_to(at_body, (TOK, 256)))
        for q in range(4):
            rest_k[k, q] = one_hot(slot == jnp.broadcast_to(at_rest, (TOK, 256)) + REST * q)
        turned_body, turned_rest = jnp.transpose(wide_body), jnp.transpose(wide_rest)
        for half in range(2):
            rows = slice(half * TOK, (half + 1) * TOK)
            here = (row + half * TOK).astype(f32)
            body_t[rows, k * TOK : (k + 1) * TOK] = one_hot(here == turned_body)
            for q in range(4):
                rest_t[q, rows, k * TOK : (k + 1) * TOK] = one_hot(here == turned_rest + REST * q)


def attend_frame(i, core, qs, ks, vs, out):
    scale = HD**-0.5
    q = qs[i]
    near = dot_nt(q, ks[i].reshape(2 * TOK, HD))
    near = jnp.where(iota((TOK, 2 * TOK), 1) // TOK <= core, near, -1e30)
    top = jnp.max(near, axis=1, keepdims=True)
    if i:
        far = dot_nt(q, ks[0:i].reshape(2 * i * TOK, HD))
        top = jnp.maximum(top, jnp.max(far, axis=1, keepdims=True))
    near = jnp.exp((near - top) * scale)
    total = jnp.sum(near, axis=1, keepdims=True)
    acc = dot(near.astype(bf16), vs[i].reshape(2 * TOK, HD))
    if i:
        far = jnp.exp((far - top) * scale)
        total = total + jnp.sum(far, axis=1, keepdims=True)
        acc = acc + dot(far.astype(bf16), vs[0:i].reshape(2 * i * TOK, HD))
    out[i] = (acc / total).astype(bf16)


def layer_kernel(
    tok_any,
    cot_any,
    action_any,
    table_any,
    gain_any,
    routes_any,
    gates_any,
    predicted_any,
    q_any,
    k_any,
    v_any,
    up_any,
    down_any,
    layer_any,
    stream_grad_any,
    up_grad_any,
    down_grad_any,
    tok,
    cot,
    action,
    table,
    gain,
    routes,
    gates,
    predicted,
    layer_out,
    stream_grad,
    up_grad,
    down_grad,
    up_w,
    down_w,
    qs,
    ks,
    vs,
    heads_out,
    attended,
    stream,
    rows,
    body_t,
    rest_t,
    body_k,
    rest_k,
    grad_send,
    grad_in,
    first_send,
    first_in,
    second_send,
    second_in,
    squares,
    inv_slots,
    pre,
    out_send,
    out_in,
    back_send,
    back_in,
    xs,
    gs,
    turned,
    act,
    act_t,
    grad_act,
    grad_pre,
    grad_norm,
    scaled_back,
    down_part,
    up_part,
    down_pair,
    up_pair,
    down_right,
    down_left,
    up_right,
    up_left,
    fetch_sem,
    result_sem,
    w_sem,
    own_sem,
    qkv_own,
    qkv_send,
    qkv_recv,
    hand_send,
    hand_recv,
    o_own,
    o_send,
    o_recv,
    x_send,
    x_recv,
    pair_send,
    pair_recv,
    ring_send,
    ring_recv,
):
    tm, ex = lax.axis_index("tm"), lax.axis_index("expert")
    chip, core = tm // 2, lax.rem(tm, 2)
    sibling = tm + 1 - 2 * core
    right, left = lax.rem(tm + 2, PEERS), lax.rem(tm + PEERS - 2, PEERS)

    def fetch(n, src, dst):
        return pltpu.make_async_copy(src, dst, fetch_sem.at[n])

    first = [
        fetch(0, routes_any, routes),
        fetch(1, gates_any, gates),
        fetch(2, predicted_any, predicted),
        fetch(3, cot_any, cot),
    ]
    later = [
        fetch(4, tok_any, tok),
        fetch(5, action_any, action),
        fetch(6, table_any, table),
        fetch(7, gain_any, gain),
    ]
    up_load = pltpu.make_async_copy(up_any, up_w, w_sem.at[0])
    down_load = pltpu.make_async_copy(down_any, down_w, w_sem.at[1])

    def columns(p):
        return pl.ds(pl.multiple_of(p * HD, HD), HD)

    def head_of(phase, t):
        return columns(phase * CHIPS + t)

    def device_of(t):
        return 2 * t + core

    def other_chip(o):
        return lax.rem(chip + o, CHIPS)

    def far_chip(s):
        half = s // 2
        return other_chip(4 + half - 2 * half * lax.rem(s, 2))

    def head_copy(n, phase, t, slot):
        src = (q_any, k_any, v_any)[n].at[:, head_of(phase, t)]
        dst = qs.at[phase, slot] if n == 0 else (ks, vs)[n - 1].at[phase, slot, core]
        return src, dst

    def head_remote(n, phase, t, slot):
        src, dst = head_copy(n, phase, t, slot)
        return remote(
            src, dst, qkv_send.at[phase, n, t], qkv_recv.at[phase, n, slot], "tm", device_of(t)
        )

    own_heads = [
        pltpu.make_async_copy(*head_copy(n, phase, chip, chip), qkv_own.at[phase, n])
        for phase in range(PHASES)
        for n in range(3)
    ]

    barrier = pltpu.get_barrier_semaphore()

    def signal(axis, peer):
        pl.semaphore_signal(barrier, inc=1, device_id={axis: peer}, device_id_type=MESH)

    signal("tm", sibling)
    each(1, CHIPS, lambda o: signal("tm", device_of(other_chip(o))))
    each(1, PEERS, lambda o: signal("expert", expert_peer(ex, o)))
    for copy in first + own_heads + later + [down_load, up_load]:
        copy.start()

    pl.semaphore_wait(barrier, CHIPS + PEERS - 1)

    def send_keys(phase):
        def go(s):
            t = far_chip(s)
            head_remote(1, phase, t, chip).start()
            head_remote(2, phase, t, chip).start()

        each(1, CHIPS, go)

    def send_queries(phase):
        each(1, CHIPS, lambda s: head_remote(0, phase, far_chip(s), chip).start())

    send_keys(0)
    send_queries(0)

    for copy in first:
        copy.wait()
    route_hots(routes, body_t, rest_t, body_k, rest_k)
    kept = turned_row(predicted, 0)[:, 0:1]
    gate = [turned_row(gates, k)[:, 0:1] for k in range(2)]
    upstream = cot[...].astype(f32) * kept
    for k in range(2):
        rows[k * TOK : (k + 1) * TOK, :] = (gate[k] * upstream).astype(bf16)
    pack(grad_send, body_t, rest_t, rows)

    exchange_start(grad_send, grad_in, x_send.at[0], x_recv.at[0], own_sem.at[0], ex)
    send_keys(1)

    for copy in own_heads:
        copy.wait()

    def hand(phase, n, which):
        ref = (ks, vs)[n].at[phase, :, which]
        return remote(ref, ref, hand_send.at[phase, n], hand_recv.at[phase, n], "tm", sibling)

    def wait_keys(phase):
        def go(o):
            t = other_chip(o)
            head_remote(1, phase, t, t).wait_recv()
            head_remote(2, phase, t, t).wait_recv()

        each(1, CHIPS, go)
        for n in range(2):
            hand(phase, n, core).start()

    def wait_handed(phase):
        for n in range(2):
            hand(phase, n, 1 - core).wait_recv()

    def head_out(phase, t, slot):
        return remote(
            heads_out.at[phase, t],
            attended.at[:, head_of(phase, slot)],
            o_send.at[phase, t],
            o_recv.at[phase, slot],
            "tm",
            device_of(t),
        )

    def own_out(phase):
        return pltpu.make_async_copy(
            heads_out.at[phase, chip], attended.at[:, head_of(phase, chip)], o_own.at[phase]
        )

    def attend(phase):
        def go(s):
            half = (s + 1) // 2
            i = lax.rem(chip + 4 + half - 2 * half * lax.rem(s, 2), CHIPS)

            @pl.when(i != chip)
            def _():
                head_remote(0, phase, i, i).wait_recv()

            lax.switch(
                i,
                [
                    functools.partial(
                        attend_frame,
                        n,
                        core,
                        qs.at[phase],
                        ks.at[phase],
                        vs.at[phase],
                        heads_out.at[phase],
                    )
                    for n in range(CHIPS)
                ],
            )

            @pl.when(i != chip)
            def _():
                head_out(phase, i, chip).start()

        each(0, CHIPS, go)
        own_out(phase).start()

    def wait_attended(phase):
        own_out(phase).wait()

        def go(o):
            t = other_chip(o)
            head_out(phase, t, t).wait_recv()

        each(1, CHIPS, go)

    def columns_done(phase):
        d = slice(phase * HALF, (phase + 1) * HALF)
        total = tok[:, d].astype(f32) + attended[:, d].astype(f32) + action_row[:, d]
        stream[:, d] = total.astype(bf16)
        held = stream[:, d].astype(f32)
        part = (held * gain[:, d]).astype(bf16)
        rows[0:TOK, 0:HALF] = part
        rows[TOK : 2 * TOK, 0:HALF] = part
        return jnp.sum(held * held, axis=1, keepdims=True)

    def turn(phase):
        for n in range(4):
            lo = phase * HALF + n * 256
            turned[phase * 4 + n] = jnp.transpose(xs[:, lo : lo + 256]).reshape(2, 128, PADDED)

    wait_keys(0)
    wait_handed(0)
    attend(0)
    send_queries(1)

    down_load.wait()
    exchange_wait(grad_send, grad_in, x_send.at[0], x_recv.at[0], own_sem.at[0], ex)
    unpack(gs, grad_in)

    def act_back(n):
        f = pl.ds(pl.multiple_of(n * 256, 256), 256)
        grad_act[:, f] = dot_nt(gs[0:ROWS, :], down_w[f, :])

    each(0, FF // 256, act_back)
    for copy in later:
        copy.wait()
    choose = one_hot(iota((8, ACTIONS), 1) == jnp.broadcast_to(action[...], (8, ACTIONS)))
    action_row = dot(choose, table[...])[0:1, :]

    wait_keys(1)
    wait_attended(0)
    squares[...] = columns_done(0)
    pack_half(first_send, body_t, rest_t, rows)
    exchange_start(first_send, first_in, x_send.at[1], x_recv.at[1], own_sem.at[1], ex)
    wait_handed(1)
    attend(1)
    wait_attended(1)

    inv_rms = lax.rsqrt((squares[...] + columns_done(1)) * (1.0 / D) + norm_eps)
    pack_half(second_send, body_t, rest_t, rows)
    lane = iota((TOK, TOK), 1)
    in_body = in_rest = jnp.zeros((TOK, TOK), f32)
    for n, part in enumerate(three_parts(inv_rms)):
        in_body = jnp.where(lane == n, part, in_body)
        in_rest = jnp.where(lane == n + 3, part, in_rest)
    in_body, in_rest = in_body.astype(bf16), in_rest.astype(bf16)
    second_send[:, HALF_BLOCK:] = (
        dot(body_t[:, 0:TOK] + body_t[:, TOK:], in_body)
        + dot(rest_t[0, :, 0:TOK] + rest_t[0, :, TOK:], in_rest)
    ).astype(bf16)
    exchange_start(second_send, second_in, x_send.at[4], x_recv.at[4], own_sem.at[4], ex)

    up_load.wait()
    exchange_wait(first_send, first_in, x_send.at[1], x_recv.at[1], own_sem.at[1], ex)
    unpack_half(xs, first_in, 0)

    def first_up(n):
        f = pl.ds(pl.multiple_of(n * 256, 256), 256)
        pre[:, f] = dot(xs[0:ROWS, 0:HALF], up_w[0:HALF, f])

    each(0, FF // 256, first_up)
    turn(0)
    exchange_wait(second_send, second_in, x_send.at[4], x_recv.at[4], own_sem.at[4], ex)
    unpack_half(xs, second_in, 1)
    parts = second_in[:, HALF_BLOCK:]
    lane = iota((256, TOK), 1)
    inv_slots[0:256, :] = jnp.sum(
        jnp.where(lane < 3, parts.astype(f32), 0.0), axis=1, keepdims=True
    )
    lane = iota((64, TOK), 1)
    inv_slots[256:ROWS, :] = jnp.sum(
        jnp.where(jnp.logical_and(lane >= 3, lane < 6), dot(rest_pick(0), parts), 0.0),
        axis=1,
        keepdims=True,
    )

    act[ROWS:PADDED, :] = jnp.zeros((PADDED - ROWS, FF), bf16)
    grad_pre[ROWS:PADDED, :] = jnp.zeros((PADDED - ROWS, FF), bf16)

    grad_norm[ROWS:PADDED, :] = jnp.zeros((PADDED - ROWS, FF), bf16)

    def expert_up(n):
        f = pl.ds(pl.multiple_of(n * 256, 256), 256)
        inv = inv_slots[...]
        v = (pre[:, f] + dot(xs[0:ROWS, HALF:D], up_w[HALF:D, f])) * inv
        th = jnp.tanh(gelu_coef * (v + 0.044715 * v * v * v))
        act[0:ROWS, f] = (0.5 * v * (1.0 + th)).astype(bf16)
        slope = 0.5 * (1.0 + th) + 0.5 * v * (1.0 - th * th) * gelu_coef * (
            1.0 + 3.0 * 0.044715 * v * v
        )
        back = grad_act[:, f] * slope
        grad_pre[0:ROWS, f] = back.astype(bf16)
        grad_norm[0:ROWS, f] = (back * inv).astype(bf16)
        act_t[pl.ds(n * 2, 2)] = jnp.transpose(act[:, f]).reshape(2, 2, 64, PADDED)

    each(0, FF // 256, expert_up)

    def down_weights(which):
        def go(n):
            d = pl.ds(pl.multiple_of(n * 512, 512), 512)
            part = dot(act_t[:, which].reshape(CHIPS * 64, PADDED), gs[:, d]).astype(bf16)
            down_part[:, which, :, d] = part.reshape(CHIPS, 64, 512)

        each(0, D // 512, go)

    def up_weights(which):
        def go(n):
            part = dot(turned[pl.ds(n * 2, 2), which].reshape(256, PADDED), grad_norm[...])
            up_part[pl.ds(n * 2, 2), which] = part.astype(bf16).reshape(2, 128, FF)

        each(0, CHIPS // 2, go)

    def pair(n, t):
        part, got = ((down_part, down_pair), (up_part, up_pair))[n]
        return remote(
            part.at[t, 1 - core], got.at[t], pair_send.at[n, t], pair_recv.at[n, t], "tm", sibling
        )

    def pair_start(n):
        for o in (7, 1, 6, 2, 5, 3, 4, 0):
            pair(n, other_chip(o)).start()

    def pair_wait(n, offsets):
        for o in offsets:
            pair(n, other_chip(o)).wait_recv()

    near_chips, far_chips = (7, 1), (6, 2, 5, 3, 4, 0)

    down_weights(1 - core)
    pair_start(0)
    turn(1)
    down_weights(core)
    up_weights(1 - core)
    pair_start(1)

    def send_rows(dst, product):
        rest = None
        for q in range(4):
            part = product(q).astype(bf16)
            dst[:, q * QUARTER : (q + 1) * QUARTER] = part[0:256, :]
            more = dot(rest_put(q), part[256:ROWS, :])
            rest = more if rest is None else rest + more
        dst[:, D:BLOCK] = rest.astype(bf16)

    streams = (
        (down_pair, down_part, down_right, 0, 32, 1, right),
        (down_pair, down_part, down_left, 32, 32, -1, left),
        (up_pair, up_part, up_right, 0, 64, 1, right),
        (up_pair, up_part, up_left, 64, 64, -1, left),
    )

    def chip_sum(n, t):
        pair, part, _, lo, size, _, _ = streams[n]
        return (
            pair[t, lo : lo + size, :].astype(f32) + part[t, core, lo : lo + size, :].astype(f32)
        )

    def hop(n, src, s):
        _, _, slots, _, _, _, to = streams[n]
        return remote(src, slots.at[s], ring_send.at[n, s], ring_recv.at[n, s], "tm", to)

    def first_hop(n):
        pair, _, _, lo, size, way, _ = streams[n]
        t = lax.rem(chip - way + CHIPS, CHIPS)
        pair[t, lo : lo + size, :] = chip_sum(n, t).astype(bf16)
        hop(n, pair.at[t, lo : lo + size, :], 0).start()

    def next_hop(n, s):
        _, _, slots, _, _, way, _ = streams[n]
        t = lax.rem(chip - way * (1 + s) + 2 * CHIPS, CHIPS)
        hop(n, slots.at[s - 1], s - 1).wait_recv()
        slots[s - 1] = (slots[s - 1].astype(f32) + chip_sum(n, t)).astype(bf16)
        hop(n, slots.at[s - 1], s).start()

    pair_wait(0, near_chips)
    first_hop(0)
    first_hop(1)
    up_weights(core)
    pair_wait(1, near_chips)
    first_hop(2)
    first_hop(3)
    send_rows(
        out_send, lambda q: dot(act[0:ROWS, :], down_w[:, q * QUARTER : (q + 1) * QUARTER])
    )
    exchange_start(out_send, out_in, x_send.at[2], x_recv.at[2], own_sem.at[2], ex)

    pair_wait(0, far_chips)
    pair_wait(1, far_chips)
    next_hop(0, 1)
    next_hop(1, 1)

    send_rows(
        back_send, lambda q: dot_nt(grad_pre[0:ROWS, :], up_w[q * QUARTER : (q + 1) * QUARTER, :])
    )
    exchange_start(back_send, back_in, x_send.at[3], x_recv.at[3], own_sem.at[3], ex)

    def hops(s):
        next_hop(2, s)
        next_hop(3, s)
        next_hop(0, s + 1)
        next_hop(1, s + 1)

    each(1, CHIPS - 2, hops)
    next_hop(2, CHIPS - 2)
    next_hop(3, CHIPS - 2)

    exchange_wait(out_send, out_in, x_send.at[2], x_recv.at[2], own_sem.at[2], ex)
    for q in range(4):
        d = slice(q * QUARTER, (q + 1) * QUARTER)
        mixed = stream[:, d].astype(f32)
        for k in range(2):
            picked = dot(body_k[k], out_in[:, d]) + dot(rest_k[k, q], out_in[:, D:BLOCK])
            mixed = mixed + gate[k] * picked
        layer_out[:, d] = mixed.astype(bf16)
    layer_store = pltpu.make_async_copy(layer_out, layer_any, result_sem.at[0])
    layer_store.start()

    exchange_wait(back_send, back_in, x_send.at[3], x_recv.at[3], own_sem.at[3], ex)
    held = stream[...].astype(f32)
    inv_rms = lax.rsqrt(jnp.mean(held * held, axis=1, keepdims=True) + norm_eps)
    both = jnp.zeros((TOK, 1), f32)
    for q in range(4):
        d = slice(q * QUARTER, (q + 1) * QUARTER)
        back = dot(body_k[0] + body_k[1], back_in[:, d]) + dot(
            rest_k[0, q] + rest_k[1, q], back_in[:, D:BLOCK]
        )
        back = back * gain[:, d]
        scaled_back[:, d] = back
        unit = stream[:, d].astype(f32) * inv_rms
        both = both + jnp.sum(back * unit, axis=1, keepdims=True)
    both = both * (1.0 / D)
    for q in range(4):
        d = slice(q * QUARTER, (q + 1) * QUARTER)
        unit = stream[:, d].astype(f32) * inv_rms
        up_here = cot[:, d].astype(f32) * kept
        stream_grad[:, d] = (up_here + inv_rms * (scaled_back[:, d] - unit * both)).astype(bf16)

    stream_store = pltpu.make_async_copy(stream_grad, stream_grad_any, result_sem.at[1])
    stream_store.start()

    def sent(o):
        t = other_chip(o)
        for phase in range(PHASES):
            for n in range(3):
                head_remote(n, phase, t, t).wait_send()
            head_out(phase, t, t).wait_send()

    each(1, CHIPS, sent)
    for phase in range(PHASES):
        for n in range(2):
            hand(phase, n, core).wait_send()
    for n, (a, b) in enumerate(
        (
            (grad_send, grad_in),
            (first_send, first_in),
            (out_send, out_in),
            (back_send, back_in),
            (second_send, second_in),
        )
    ):
        exchange_sent(a, b, x_send.at[n], x_recv.at[n], ex)

    def pairs_sent(t):
        pair(0, t).wait_send()
        pair(1, t).wait_send()

    each(0, CHIPS, pairs_sent)

    for n, out in ((0, down_grad), (1, down_grad), (2, up_grad), (3, up_grad)):
        _, _, slots, lo, size, _, _ = streams[n]
        hop(n, slots.at[CHIPS - 2], CHIPS - 2).wait_recv()
        out[lo : lo + size, :] = (slots[CHIPS - 2].astype(f32) + chip_sum(n, chip)).astype(bf16)

    up_store = pltpu.make_async_copy(up_grad, up_grad_any, result_sem.at[2])
    down_store = pltpu.make_async_copy(down_grad, down_grad_any, result_sem.at[3])
    up_store.start()
    down_store.start()

    def hops_sent(s):
        for n, (_, _, slots, _, _, _, _) in enumerate(streams):
            hop(n, slots.at[s], s).wait_send()

    each(0, CHIPS - 1, hops_sent)
    for copy in (layer_store, stream_store, up_store, down_store):
        copy.wait()


def deliver_kernel(*refs):
    made, given, held, came, left = refs[0:4], refs[4:8], refs[8:12], refs[12], refs[13]
    inward = [pltpu.make_async_copy(made[n], held[n], came.at[n]) for n in range(4)]
    outward = [pltpu.make_async_copy(held[n], given[n], left.at[n]) for n in range(4)]
    for copy in inward:
        copy.start()
    for n in range(4):
        inward[n].wait()
        outward[n].start()
    for copy in outward:
        copy.wait()


def local(
    tokens,
    queries,
    key_rows,
    values,
    actions,
    action_table,
    norm_gain,
    routes,
    gate_probs,
    predicted,
    cotangent,
    up_weight,
    down_weight,
):
    hbm = pl.BlockSpec(memory_space=pl.ANY)
    dma = pltpu.SemaphoreType.DMA
    block = pltpu.VMEM((256, BLOCK), bf16)
    results = (
        jax.ShapeDtypeStruct((TOK, D), bf16),
        jax.ShapeDtypeStruct((TOK, D), bf16),
        jax.ShapeDtypeStruct((D // PEERS, FF), bf16),
        jax.ShapeDtypeStruct((FF // PEERS, D), bf16),
    )
    made = pl.pallas_call(
        layer_kernel,
        out_shape=results,
        in_specs=[hbm] * 13,
        out_specs=(hbm,) * 4,
        scratch_shapes=[
            pltpu.VMEM((TOK, D), bf16),
            pltpu.VMEM((TOK, D), bf16),
            pltpu.VMEM((1, 1), jnp.int32),
            pltpu.VMEM((ACTIONS, D), bf16),
            pltpu.VMEM((1, D), f32),
            pltpu.VMEM((2, TOK), jnp.int32),
            pltpu.VMEM((2, TOK), f32),
            pltpu.VMEM((1, TOK), jnp.int32),
            pltpu.VMEM((TOK, D), bf16),
            pltpu.VMEM((TOK, D), bf16),
            pltpu.VMEM((D // PEERS, FF), bf16),
            pltpu.VMEM((FF // PEERS, D), bf16),
            pltpu.VMEM((D, FF), bf16),
            pltpu.VMEM((FF, D), bf16),
            pltpu.VMEM((PHASES, CHIPS, TOK, HD), bf16),
            pltpu.VMEM((PHASES, CHIPS, 2, TOK, HD), bf16),
            pltpu.VMEM((PHASES, CHIPS, 2, TOK, HD), bf16),
            pltpu.VMEM((PHASES, CHIPS, TOK, HD), bf16),
            pltpu.VMEM((TOK, D), bf16),
            pltpu.VMEM((TOK, D), bf16),
            pltpu.VMEM((2 * TOK, D), bf16),
            pltpu.VMEM((256, 256), bf16),
            pltpu.VMEM((4, 256, 256), bf16),
            pltpu.VMEM((2, TOK, 256), bf16),
            pltpu.VMEM((2, 4, TOK, 256), bf16),
        ]
        + [block] * 2
        + [
            pltpu.VMEM((256, HALF_BLOCK), bf16),
            pltpu.VMEM((256, HALF_BLOCK), bf16),
            pltpu.VMEM((256, HALF_BLOCK + TOK), bf16),
            pltpu.VMEM((256, HALF_BLOCK + TOK), bf16),
            pltpu.VMEM((TOK, 1), f32),
            pltpu.VMEM((ROWS, 1), f32),
            pltpu.VMEM((ROWS, FF), f32),
        ]
        + [block] * 4
        + [
            pltpu.VMEM((PADDED, D), bf16),
            pltpu.VMEM((PADDED, D), bf16),
            pltpu.VMEM((CHIPS, 2, 128, PADDED), bf16),
            pltpu.VMEM((PADDED, FF), bf16),
            pltpu.VMEM((CHIPS, 2, 64, PADDED), bf16),
            pltpu.VMEM((ROWS, FF), f32),
            pltpu.VMEM((PADDED, FF), bf16),
            pltpu.VMEM((PADDED, FF), bf16),
            pltpu.VMEM((TOK, D), f32),
            pltpu.VMEM((CHIPS, 2, 64, D), bf16),
            pltpu.VMEM((CHIPS, 2, 128, FF), bf16),
            pltpu.VMEM((CHIPS, 64, D), bf16),
            pltpu.VMEM((CHIPS, 128, FF), bf16),
            pltpu.VMEM((CHIPS - 1, 32, D), bf16),
            pltpu.VMEM((CHIPS - 1, 32, D), bf16),
            pltpu.VMEM((CHIPS - 1, 64, FF), bf16),
            pltpu.VMEM((CHIPS - 1, 64, FF), bf16),
            dma((8,)),
            dma((4,)),
            dma((2,)),
            dma((5,)),
            dma((PHASES, 3)),
            dma((PHASES, 3, CHIPS)),
            dma((PHASES, 3, CHIPS)),
            dma((PHASES, 2)),
            dma((PHASES, 2)),
            dma((PHASES,)),
            dma((PHASES, CHIPS)),
            dma((PHASES, CHIPS)),
            dma((5, PEERS)),
            dma((5, PEERS)),
            dma((2, CHIPS)),
            dma((2, CHIPS)),
            dma((4, CHIPS - 1)),
            dma((4, CHIPS - 1)),
        ],
        compiler_params=pltpu.CompilerParams(
            collective_id=0, has_side_effects=True, vmem_limit_bytes=62 * 2**20
        ),
        name="layer",
    )(
        tokens.reshape(TOK, D),
        cotangent.reshape(TOK, D),
        actions,
        action_table,
        norm_gain.reshape(1, D),
        routes.reshape(TOK, 2).T,
        gate_probs.reshape(TOK, 2).T,
        predicted.reshape(1, TOK),
        queries.reshape(TOK, D),
        key_rows.reshape(TOK, D),
        values.reshape(TOK, D),
        up_weight.reshape(D, FF),
        down_weight.reshape(FF, D),
    )
    layer_out, stream_grad, up_grad, down_grad = pl.pallas_call(
        deliver_kernel,
        out_shape=results,
        in_specs=[hbm] * 4,
        out_specs=(hbm,) * 4,
        scratch_shapes=[pltpu.VMEM(r.shape, r.dtype) for r in results] + [dma((4,)), dma((4,))],
        name="deliver",
    )(*made)
    return (
        layer_out.reshape(tokens.shape),
        stream_grad.reshape(tokens.shape),
        up_grad.reshape(1, D // PEERS, FF),
        down_grad.reshape(1, FF // PEERS, D),
    )


def solution(mesh):
    rows = P("expert", "tm", None, None)
    in_specs = (
        rows,
        rows,
        rows,
        rows,
        P("expert", "tm"),
        P(),
        P(),
        rows,
        rows,
        P("expert", "tm", None),
        rows,
        P("expert", None, None),
        P("expert", None, None),
    )
    out_specs = (rows, rows, P("expert", "tm", None), P("expert", "tm", None))
    return jax.shard_map(local, mesh=mesh, in_specs=in_specs, out_specs=out_specs, check_vma=False)
```

```python
import functools

import jax
import jax.numpy as jnp
from jax import lax
from jax.experimental import pallas as pl
from jax.experimental.pallas import tpu as pltpu
from jax.sharding import PartitionSpec as P

MESH = pl.DeviceIdType.MESH
PEERS = 16
HEADS = 16
HD = 128
D = 2048
FF = 1024
ACTIONS = 64
TOK = 128
CHIPS = 8
BODY = 16
REST = 4
ROWS = 320
PADDED = 384
QUARTER = 512
BLOCK = D + QUARTER
HALF = D // 2
PIECE = HALF // 4
HALF_BLOCK = HALF + PIECE
PHASES = 2

norm_eps = 1e-06
gelu_coef = 0.7978845608028654

f32 = jnp.float32
bf16 = jnp.bfloat16


def dot(a, b):
    return jnp.dot(a, b, preferred_element_type=f32)


def dot_nt(a, b):
    return lax.dot_general(a, b, (((1,), (1,)), ((), ())), preferred_element_type=f32)


def iota(shape, dim):
    return lax.broadcasted_iota(jnp.int32, shape, dim)


def one_hot(mask):
    return mask.astype(f32).astype(bf16)


def tm_peer(me, o):
    return lax.rem(me + o, PEERS)


def expert_peer(me, o):
    y, x = me // 4, lax.rem(me, 4)
    return lax.rem(y + o // 4, 4) * 4 + lax.rem(x + lax.rem(o, 4), 4)


FAR_FIRST = (10, 2, 8, 6, 14, 9, 11, 5, 7, 13, 15, 1, 3, 4, 12)


def far_first(s):
    half = s // 2
    return 8 + half - 2 * half * lax.rem(s, 2)


def remote(src, dst, send, recv, axis, peer):
    return pltpu.make_async_remote_copy(
        src_ref=src,
        dst_ref=dst,
        send_sem=send,
        recv_sem=recv,
        device_id={axis: peer},
        device_id_type=MESH,
    )


def each(lo, hi, fn):
    def body(s, c):
        fn(s)
        return c

    lax.fori_loop(lo, hi, body, 0)


def rows_of(p):
    return pl.ds(pl.multiple_of(p * BODY, BODY), BODY)


def exchange_start(src, dst, send, recv, own, me):
    def go(o):
        p = expert_peer(me, o)
        remote(
            src.at[rows_of(p), :], dst.at[rows_of(me), :], send.at[p], recv.at[me], "expert", p
        ).start()

    for o in FAR_FIRST:
        go(o)
    pltpu.make_async_copy(src.at[rows_of(me), :], dst.at[rows_of(me), :], own).start()


def exchange_wait(src, dst, send, recv, own, me):
    pltpu.make_async_copy(src.at[rows_of(me), :], dst.at[rows_of(me), :], own).wait()

    def go(o):
        p = expert_peer(me, o)
        remote(
            src.at[rows_of(p), :], dst.at[rows_of(p), :], send.at[p], recv.at[p], "expert", p
        ).wait_recv()

    each(1, PEERS, go)


def exchange_sent(src, dst, send, recv, me):
    def go(o):
        p = expert_peer(me, o)
        remote(
            src.at[rows_of(p), :], dst.at[rows_of(p), :], send.at[p], recv.at[p], "expert", p
        ).wait_send()

    each(1, PEERS, go)


def pack(dst, body_hot, rest_hot, src):
    rest = None
    for q in range(4):
        part = src[:, q * QUARTER : (q + 1) * QUARTER]
        dst[:, q * QUARTER : (q + 1) * QUARTER] = dot(body_hot[...], part).astype(bf16)
        more = dot(rest_hot[q], part)
        rest = more if rest is None else rest + more
    dst[:, D:BLOCK] = rest.astype(bf16)


def pack_half(dst, body_hot, rest_hot, src):
    for q in range(2):
        d = slice(q * QUARTER, (q + 1) * QUARTER)
        dst[:, d] = dot(body_hot[...], src[:, d]).astype(bf16)
    rest = None
    for q in range(4):
        more = dot(rest_hot[q], src[:, q * PIECE : (q + 1) * PIECE])
        rest = more if rest is None else rest + more
    dst[:, HALF:HALF_BLOCK] = rest.astype(bf16)


def rest_pick(q):
    i, j = iota((64, 256), 0), iota((64, 256), 1)
    return one_hot(j == (i // REST) * BODY + q * REST + lax.rem(i, REST))


def rest_put(q):
    j, i = iota((256, 64), 0), iota((256, 64), 1)
    return one_hot(j == (i // REST) * BODY + q * REST + lax.rem(i, REST))


def unpack(dst, src):
    dst[0:256, :] = src[:, 0:D]
    for q in range(4):
        dst[256:ROWS, q * QUARTER : (q + 1) * QUARTER] = dot(rest_pick(q), src[:, D:BLOCK]).astype(
            bf16
        )
    dst[ROWS:PADDED, :] = jnp.zeros((PADDED - ROWS, D), bf16)


def turned_row(ref, k):
    return jnp.transpose(jnp.broadcast_to(ref[k : k + 1, :].astype(f32), (TOK, TOK)))


def unpack_half(dst, src, phase):
    lo = phase * HALF
    dst[0:256, lo : lo + HALF] = src[:, 0:HALF]
    for q in range(4):
        at = lo + q * PIECE
        dst[256:ROWS, at : at + PIECE] = dot(rest_pick(q), src[:, HALF:HALF_BLOCK]).astype(bf16)
    dst[ROWS:PADDED, lo : lo + HALF] = jnp.zeros((PADDED - ROWS, HALF), bf16)


def three_parts(v):
    high = v.astype(bf16)
    low = v - high.astype(f32)
    middle = low.astype(bf16)
    return high.astype(f32), middle.astype(f32), low - middle.astype(f32)


def route_hots(routes, body_t, rest_t, body_k, rest_k):
    lane, row = iota((TOK, TOK), 1), iota((TOK, TOK), 0)
    r = [turned_row(routes, k) for k in range(2)]
    hit = [lane.astype(f32) == r[k] for k in range(2)]
    hits = one_hot(jnp.logical_or(hit[0], hit[1]))
    rank = dot(one_hot(lane < row), hits)
    for k in range(2):
        mine = jnp.sum(jnp.where(hit[k], rank, 0.0), axis=1, keepdims=True)
        base = r[k][:, 0:1] * BODY + mine
        at_body = jnp.where(mine < BODY, base, -1.0)
        at_rest = jnp.where(mine < BODY, -1000.0, base - BODY)
        wide_body = jnp.broadcast_to(at_body, (TOK, TOK))
        wide_rest = jnp.broadcast_to(at_rest, (TOK, TOK))
        slot = iota((TOK, 256), 1).astype(f32)
        body_k[k] = one_hot(slot == jnp.broadcast_to(at_body, (TOK, 256)))
        for q in range(4):
            rest_k[k, q] = one_hot(slot == jnp.broadcast_to(at_rest, (TOK, 256)) + REST * q)
        turned_body, turned_rest = jnp.transpose(wide_body), jnp.transpose(wide_rest)
        for half in range(2):
            rows = slice(half * TOK, (half + 1) * TOK)
            here = (row + half * TOK).astype(f32)
            body_t[rows, k * TOK : (k + 1) * TOK] = one_hot(here == turned_body)
            for q in range(4):
                rest_t[q, rows, k * TOK : (k + 1) * TOK] = one_hot(here == turned_rest + REST * q)


def attend_frame(i, core, qs, ks, vs, out):
    scale = HD**-0.5
    q = qs[i]
    near = dot_nt(q, ks[i].reshape(2 * TOK, HD))
    near = jnp.where(iota((TOK, 2 * TOK), 1) // TOK <= core, near, -1e30)
    top = jnp.max(near, axis=1, keepdims=True)
    if i:
        far = dot_nt(q, ks[0:i].reshape(2 * i * TOK, HD))
        top = jnp.maximum(top, jnp.max(far, axis=1, keepdims=True))
    near = jnp.exp((near - top) * scale)
    total = jnp.sum(near, axis=1, keepdims=True)
    acc = dot(near.astype(bf16), vs[i].reshape(2 * TOK, HD))
    if i:
        far = jnp.exp((far - top) * scale)
        total = total + jnp.sum(far, axis=1, keepdims=True)
        acc = acc + dot(far.astype(bf16), vs[0:i].reshape(2 * i * TOK, HD))
    out[i] = (acc / total).astype(bf16)


def layer_kernel(
    tok_any,
    cot_any,
    action_any,
    table_any,
    gain_any,
    routes_any,
    gates_any,
    predicted_any,
    q_any,
    k_any,
    v_any,
    up_any,
    down_any,
    layer_any,
    stream_grad_any,
    up_grad_any,
    down_grad_any,
    tok,
    cot,
    action,
    table,
    gain,
    routes,
    gates,
    predicted,
    layer_out,
    stream_grad,
    up_grad,
    down_grad,
    up_w,
    down_w,
    qs,
    ks,
    vs,
    heads_out,
    attended,
    stream,
    rows,
    body_t,
    rest_t,
    body_k,
    rest_k,
    grad_send,
    grad_in,
    first_send,
    first_in,
    second_send,
    second_in,
    squares,
    inv_slots,
    pre,
    out_send,
    out_in,
    back_send,
    back_in,
    xs,
    gs,
    turned,
    act,
    act_t,
    grad_act,
    grad_pre,
    grad_norm,
    scaled_back,
    down_part,
    up_part,
    down_pair,
    up_pair,
    down_right,
    down_left,
    up_right,
    up_left,
    fetch_sem,
    result_sem,
    w_sem,
    own_sem,
    qkv_own,
    qkv_send,
    qkv_recv,
    hand_send,
    hand_recv,
    o_own,
    o_send,
    o_recv,
    x_send,
    x_recv,
    pair_send,
    pair_recv,
    ring_send,
    ring_recv,
):
    tm, ex = lax.axis_index("tm"), lax.axis_index("expert")
    chip, core = tm // 2, lax.rem(tm, 2)
    sibling = tm + 1 - 2 * core
    right, left = lax.rem(tm + 2, PEERS), lax.rem(tm + PEERS - 2, PEERS)

    def fetch(n, src, dst):
        return pltpu.make_async_copy(src, dst, fetch_sem.at[n])

    first = [
        fetch(0, routes_any, routes),
        fetch(1, gates_any, gates),
        fetch(2, predicted_any, predicted),
        fetch(3, cot_any, cot),
    ]
    later = [
        fetch(4, tok_any, tok),
        fetch(5, action_any, action),
        fetch(6, table_any, table),
        fetch(7, gain_any, gain),
    ]
    up_load = pltpu.make_async_copy(up_any, up_w, w_sem.at[0])
    down_load = pltpu.make_async_copy(down_any, down_w, w_sem.at[1])

    def columns(p):
        return pl.ds(pl.multiple_of(p * HD, HD), HD)

    def head_of(phase, t):
        return columns(phase * CHIPS + t)

    def device_of(t):
        return 2 * t + core

    def other_chip(o):
        return lax.rem(chip + o, CHIPS)

    def far_chip(s):
        half = s // 2
        return other_chip(4 + half - 2 * half * lax.rem(s, 2))

    def head_copy(n, phase, t, slot):
        src = (q_any, k_any, v_any)[n].at[:, head_of(phase, t)]
        dst = qs.at[phase, slot] if n == 0 else (ks, vs)[n - 1].at[phase, slot, core]
        return src, dst

    def head_remote(n, phase, t, slot):
        src, dst = head_copy(n, phase, t, slot)
        return remote(
            src, dst, qkv_send.at[phase, n, t], qkv_recv.at[phase, n, slot], "tm", device_of(t)
        )

    own_heads = [
        pltpu.make_async_copy(*head_copy(n, phase, chip, chip), qkv_own.at[phase, n])
        for phase in range(PHASES)
        for n in range(3)
    ]

    barrier = pltpu.get_barrier_semaphore()

    def signal(axis, peer):
        pl.semaphore_signal(barrier, inc=1, device_id={axis: peer}, device_id_type=MESH)

    signal("tm", sibling)
    each(1, CHIPS, lambda o: signal("tm", device_of(other_chip(o))))
    each(1, PEERS, lambda o: signal("expert", expert_peer(ex, o)))
    for copy in first + own_heads + later + [down_load, up_load]:
        copy.start()

    pl.semaphore_wait(barrier, CHIPS + PEERS - 1)

    def send_keys(phase):
        def go(s):
            t = far_chip(s)
            head_remote(1, phase, t, chip).start()
            head_remote(2, phase, t, chip).start()

        each(1, CHIPS, go)

    def send_queries(phase):
        each(1, CHIPS, lambda s: head_remote(0, phase, far_chip(s), chip).start())

    send_keys(0)
    send_queries(0)

    for copy in first:
        copy.wait()
    route_hots(routes, body_t, rest_t, body_k, rest_k)
    kept = turned_row(predicted, 0)[:, 0:1]
    gate = [turned_row(gates, k)[:, 0:1] for k in range(2)]
    upstream = cot[...].astype(f32) * kept
    for k in range(2):
        rows[k * TOK : (k + 1) * TOK, :] = (gate[k] * upstream).astype(bf16)
    pack(grad_send, body_t, rest_t, rows)

    exchange_start(grad_send, grad_in, x_send.at[0], x_recv.at[0], own_sem.at[0], ex)
    send_keys(1)

    for copy in own_heads:
        copy.wait()

    def hand(phase, n, which):
        ref = (ks, vs)[n].at[phase, :, which]
        return remote(ref, ref, hand_send.at[phase, n], hand_recv.at[phase, n], "tm", sibling)

    def wait_keys(phase):
        def go(o):
            t = other_chip(o)
            head_remote(1, phase, t, t).wait_recv()
            head_remote(2, phase, t, t).wait_recv()

        each(1, CHIPS, go)
        for n in range(2):
            hand(phase, n, core).start()

    def wait_handed(phase):
        for n in range(2):
            hand(phase, n, 1 - core).wait_recv()

    def head_out(phase, t, slot):
        return remote(
            heads_out.at[phase, t],
            attended.at[:, head_of(phase, slot)],
            o_send.at[phase, t],
            o_recv.at[phase, slot],
            "tm",
            device_of(t),
        )

    def own_out(phase):
        return pltpu.make_async_copy(
            heads_out.at[phase, chip], attended.at[:, head_of(phase, chip)], o_own.at[phase]
        )

    def attend(phase):
        def go(s):
            half = (s + 1) // 2
            i = lax.rem(chip + 4 + half - 2 * half * lax.rem(s, 2), CHIPS)

            @pl.when(i != chip)
            def _():
                head_remote(0, phase, i, i).wait_recv()

            lax.switch(
                i,
                [
                    functools.partial(
                        attend_frame,
                        n,
                        core,
                        qs.at[phase],
                        ks.at[phase],
                        vs.at[phase],
                        heads_out.at[phase],
                    )
                    for n in range(CHIPS)
                ],
            )

            @pl.when(i != chip)
            def _():
                head_out(phase, i, chip).start()

        each(0, CHIPS, go)
        own_out(phase).start()

    def wait_attended(phase):
        own_out(phase).wait()

        def go(o):
            t = other_chip(o)
            head_out(phase, t, t).wait_recv()

        each(1, CHIPS, go)

    def columns_done(phase):
        d = slice(phase * HALF, (phase + 1) * HALF)
        total = tok[:, d].astype(f32) + attended[:, d].astype(f32) + action_row[:, d]
        stream[:, d] = total.astype(bf16)
        held = stream[:, d].astype(f32)
        part = (held * gain[:, d]).astype(bf16)
        rows[0:TOK, 0:HALF] = part
        rows[TOK : 2 * TOK, 0:HALF] = part
        return jnp.sum(held * held, axis=1, keepdims=True)

    def turn(phase):
        for n in range(4):
            lo = phase * HALF + n * 256
            turned[phase * 4 + n] = jnp.transpose(xs[:, lo : lo + 256]).reshape(2, 128, PADDED)

    wait_keys(0)
    wait_handed(0)
    attend(0)
    send_queries(1)

    down_load.wait()
    exchange_wait(grad_send, grad_in, x_send.at[0], x_recv.at[0], own_sem.at[0], ex)
    unpack(gs, grad_in)

    def act_back(n):
        f = pl.ds(pl.multiple_of(n * 256, 256), 256)
        grad_act[:, f] = dot_nt(gs[0:ROWS, :], down_w[f, :])

    each(0, FF // 256, act_back)
    for copy in later:
        copy.wait()
    choose = one_hot(iota((8, ACTIONS), 1) == jnp.broadcast_to(action[...], (8, ACTIONS)))
    action_row = dot(choose, table[...])[0:1, :]

    wait_keys(1)
    wait_attended(0)
    squares[...] = columns_done(0)
    pack_half(first_send, body_t, rest_t, rows)
    exchange_start(first_send, first_in, x_send.at[1], x_recv.at[1], own_sem.at[1], ex)
    wait_handed(1)
    attend(1)
    wait_attended(1)

    inv_rms = lax.rsqrt((squares[...] + columns_done(1)) * (1.0 / D) + norm_eps)
    pack_half(second_send, body_t, rest_t, rows)
    lane = iota((TOK, TOK), 1)
    in_body = in_rest = jnp.zeros((TOK, TOK), f32)
    for n, part in enumerate(three_parts(inv_rms)):
        in_body = jnp.where(lane == n, part, in_body)
        in_rest = jnp.where(lane == n + 3, part, in_rest)
    in_body, in_rest = in_body.astype(bf16), in_rest.astype(bf16)
    second_send[:, HALF_BLOCK:] = (
        dot(body_t[:, 0:TOK] + body_t[:, TOK:], in_body)
        + dot(rest_t[0, :, 0:TOK] + rest_t[0, :, TOK:], in_rest)
    ).astype(bf16)
    exchange_start(second_send, second_in, x_send.at[4], x_recv.at[4], own_sem.at[4], ex)

    up_load.wait()
    exchange_wait(first_send, first_in, x_send.at[1], x_recv.at[1], own_sem.at[1], ex)
    unpack_half(xs, first_in, 0)

    def first_up(n):
        f = pl.ds(pl.multiple_of(n * 256, 256), 256)
        pre[:, f] = dot(xs[0:ROWS, 0:HALF], up_w[0:HALF, f])

    each(0, FF // 256, first_up)
    turn(0)
    exchange_wait(second_send, second_in, x_send.at[4], x_recv.at[4], own_sem.at[4], ex)
    unpack_half(xs, second_in, 1)
    parts = second_in[:, HALF_BLOCK:]
    lane = iota((256, TOK), 1)
    inv_slots[0:256, :] = jnp.sum(
        jnp.where(lane < 3, parts.astype(f32), 0.0), axis=1, keepdims=True
    )
    lane = iota((64, TOK), 1)
    inv_slots[256:ROWS, :] = jnp.sum(
        jnp.where(jnp.logical_and(lane >= 3, lane < 6), dot(rest_pick(0), parts), 0.0),
        axis=1,
        keepdims=True,
    )

    act[ROWS:PADDED, :] = jnp.zeros((PADDED - ROWS, FF), bf16)
    grad_pre[ROWS:PADDED, :] = jnp.zeros((PADDED - ROWS, FF), bf16)

    grad_norm[ROWS:PADDED, :] = jnp.zeros((PADDED - ROWS, FF), bf16)

    def expert_up(n):
        f = pl.ds(pl.multiple_of(n * 256, 256), 256)
        inv = inv_slots[...]
        v = (pre[:, f] + dot(xs[0:ROWS, HALF:D], up_w[HALF:D, f])) * inv
        th = jnp.tanh(gelu_coef * (v + 0.044715 * v * v * v))
        act[0:ROWS, f] = (0.5 * v * (1.0 + th)).astype(bf16)
        slope = 0.5 * (1.0 + th) + 0.5 * v * (1.0 - th * th) * gelu_coef * (
            1.0 + 3.0 * 0.044715 * v * v
        )
        back = grad_act[:, f] * slope
        grad_pre[0:ROWS, f] = back.astype(bf16)
        grad_norm[0:ROWS, f] = (back * inv).astype(bf16)
        act_t[pl.ds(n * 2, 2)] = jnp.transpose(act[:, f]).reshape(2, 2, 64, PADDED)

    each(0, FF // 256, expert_up)

    def down_weights(which):
        def go(n):
            d = pl.ds(pl.multiple_of(n * 512, 512), 512)
            part = dot(act_t[:, which].reshape(CHIPS * 64, PADDED), gs[:, d]).astype(bf16)
            down_part[:, which, :, d] = part.reshape(CHIPS, 64, 512)

        each(0, D // 512, go)

    def up_weights(which):
        def go(n):
            part = dot(turned[pl.ds(n * 2, 2), which].reshape(256, PADDED), grad_norm[...])
            up_part[pl.ds(n * 2, 2), which] = part.astype(bf16).reshape(2, 128, FF)

        each(0, CHIPS // 2, go)

    def pair(n, t):
        part, got = ((down_part, down_pair), (up_part, up_pair))[n]
        return remote(
            part.at[t, 1 - core], got.at[t], pair_send.at[n, t], pair_recv.at[n, t], "tm", sibling
        )

    def pair_start(n):
        for o in (7, 1, 6, 2, 5, 3, 4, 0):
            pair(n, other_chip(o)).start()

    def pair_wait(n, offsets):
        for o in offsets:
            pair(n, other_chip(o)).wait_recv()

    near_chips, far_chips = (7, 1), (6, 2, 5, 3, 4, 0)

    down_weights(1 - core)
    pair_start(0)
    down_weights(core)

    def send_rows(dst, product):
        rest = None
        for q in range(4):
            part = product(q).astype(bf16)
            dst[:, q * QUARTER : (q + 1) * QUARTER] = part[0:256, :]
            more = dot(rest_put(q), part[256:ROWS, :])
            rest = more if rest is None else rest + more
        dst[:, D:BLOCK] = rest.astype(bf16)

    streams = (
        (down_pair, down_part, down_right, 0, 32, 1, right),
        (down_pair, down_part, down_left, 32, 32, -1, left),
        (up_pair, up_part, up_right, 0, 64, 1, right),
        (up_pair, up_part, up_left, 64, 64, -1, left),
    )

    def chip_sum(n, t):
        pair, part, _, lo, size, _, _ = streams[n]
        return (
            pair[t, lo : lo + size, :].astype(f32) + part[t, core, lo : lo + size, :].astype(f32)
        )

    def hop(n, src, s):
        _, _, slots, _, _, _, to = streams[n]
        return remote(src, slots.at[s], ring_send.at[n, s], ring_recv.at[n, s], "tm", to)

    def first_hop(n):
        pair, _, _, lo, size, way, _ = streams[n]
        t = lax.rem(chip - way + CHIPS, CHIPS)
        pair[t, lo : lo + size, :] = chip_sum(n, t).astype(bf16)
        hop(n, pair.at[t, lo : lo + size, :], 0).start()

    def next_hop(n, s):
        _, _, slots, _, _, way, _ = streams[n]
        t = lax.rem(chip - way * (1 + s) + 2 * CHIPS, CHIPS)
        hop(n, slots.at[s - 1], s - 1).wait_recv()
        slots[s - 1] = (slots[s - 1].astype(f32) + chip_sum(n, t)).astype(bf16)
        hop(n, slots.at[s - 1], s).start()

    pair_wait(0, near_chips)
    first_hop(0)
    first_hop(1)
    turn(1)
    up_weights(1 - core)
    pair_start(1)
    up_weights(core)
    pair_wait(1, near_chips)
    first_hop(2)
    first_hop(3)
    send_rows(
        out_send, lambda q: dot(act[0:ROWS, :], down_w[:, q * QUARTER : (q + 1) * QUARTER])
    )
    exchange_start(out_send, out_in, x_send.at[2], x_recv.at[2], own_sem.at[2], ex)

    pair_wait(0, far_chips)
    pair_wait(1, far_chips)
    next_hop(0, 1)
    next_hop(1, 1)

    send_rows(
        back_send, lambda q: dot_nt(grad_pre[0:ROWS, :], up_w[q * QUARTER : (q + 1) * QUARTER, :])
    )
    exchange_start(back_send, back_in, x_send.at[3], x_recv.at[3], own_sem.at[3], ex)

    def hops(s):
        next_hop(2, s)
        next_hop(3, s)
        next_hop(0, s + 1)
        next_hop(1, s + 1)

    each(1, CHIPS - 2, hops)
    next_hop(2, CHIPS - 2)
    next_hop(3, CHIPS - 2)

    exchange_wait(out_send, out_in, x_send.at[2], x_recv.at[2], own_sem.at[2], ex)
    for q in range(4):
        d = slice(q * QUARTER, (q + 1) * QUARTER)
        mixed = stream[:, d].astype(f32)
        for k in range(2):
            picked = dot(body_k[k], out_in[:, d]) + dot(rest_k[k, q], out_in[:, D:BLOCK])
            mixed = mixed + gate[k] * picked
        layer_out[:, d] = mixed.astype(bf16)
    layer_store = pltpu.make_async_copy(layer_out, layer_any, result_sem.at[0])
    layer_store.start()

    exchange_wait(back_send, back_in, x_send.at[3], x_recv.at[3], own_sem.at[3], ex)
    held = stream[...].astype(f32)
    inv_rms = lax.rsqrt(jnp.mean(held * held, axis=1, keepdims=True) + norm_eps)
    both = jnp.zeros((TOK, 1), f32)
    for q in range(4):
        d = slice(q * QUARTER, (q + 1) * QUARTER)
        back = dot(body_k[0] + body_k[1], back_in[:, d]) + dot(
            rest_k[0, q] + rest_k[1, q], back_in[:, D:BLOCK]
        )
        back = back * gain[:, d]
        scaled_back[:, d] = back
        unit = stream[:, d].astype(f32) * inv_rms
        both = both + jnp.sum(back * unit, axis=1, keepdims=True)
    both = both * (1.0 / D)
    for q in range(4):
        d = slice(q * QUARTER, (q + 1) * QUARTER)
        unit = stream[:, d].astype(f32) * inv_rms
        up_here = cot[:, d].astype(f32) * kept
        stream_grad[:, d] = (up_here + inv_rms * (scaled_back[:, d] - unit * both)).astype(bf16)

    stream_store = pltpu.make_async_copy(stream_grad, stream_grad_any, result_sem.at[1])
    stream_store.start()

    def sent(o):
        t = other_chip(o)
        for phase in range(PHASES):
            for n in range(3):
                head_remote(n, phase, t, t).wait_send()
            head_out(phase, t, t).wait_send()

    each(1, CHIPS, sent)
    for phase in range(PHASES):
        for n in range(2):
            hand(phase, n, core).wait_send()
    for n, (a, b) in enumerate(
        (
            (grad_send, grad_in),
            (first_send, first_in),
            (out_send, out_in),
            (back_send, back_in),
            (second_send, second_in),
        )
    ):
        exchange_sent(a, b, x_send.at[n], x_recv.at[n], ex)

    def pairs_sent(t):
        pair(0, t).wait_send()
        pair(1, t).wait_send()

    each(0, CHIPS, pairs_sent)

    for n, out in ((0, down_grad), (1, down_grad), (2, up_grad), (3, up_grad)):
        _, _, slots, lo, size, _, _ = streams[n]
        hop(n, slots.at[CHIPS - 2], CHIPS - 2).wait_recv()
        out[lo : lo + size, :] = (slots[CHIPS - 2].astype(f32) + chip_sum(n, chip)).astype(bf16)

    up_store = pltpu.make_async_copy(up_grad, up_grad_any, result_sem.at[2])
    down_store = pltpu.make_async_copy(down_grad, down_grad_any, result_sem.at[3])
    up_store.start()
    down_store.start()

    def hops_sent(s):
        for n, (_, _, slots, _, _, _, _) in enumerate(streams):
            hop(n, slots.at[s], s).wait_send()

    each(0, CHIPS - 1, hops_sent)
    for copy in (layer_store, stream_store, up_store, down_store):
        copy.wait()


def deliver_kernel(*refs):
    made, given, held, came, left = refs[0:4], refs[4:8], refs[8:12], refs[12], refs[13]
    inward = [pltpu.make_async_copy(made[n], held[n], came.at[n]) for n in range(4)]
    outward = [pltpu.make_async_copy(held[n], given[n], left.at[n]) for n in range(4)]
    for copy in inward:
        copy.start()
    for n in range(4):
        inward[n].wait()
        outward[n].start()
    for copy in outward:
        copy.wait()


def local(
    tokens,
    queries,
    key_rows,
    values,
    actions,
    action_table,
    norm_gain,
    routes,
    gate_probs,
    predicted,
    cotangent,
    up_weight,
    down_weight,
):
    hbm = pl.BlockSpec(memory_space=pl.ANY)
    dma = pltpu.SemaphoreType.DMA
    block = pltpu.VMEM((256, BLOCK), bf16)
    results = (
        jax.ShapeDtypeStruct((TOK, D), bf16),
        jax.ShapeDtypeStruct((TOK, D), bf16),
        jax.ShapeDtypeStruct((D // PEERS, FF), bf16),
        jax.ShapeDtypeStruct((FF // PEERS, D), bf16),
    )
    made = pl.pallas_call(
        layer_kernel,
        out_shape=results,
        in_specs=[hbm] * 13,
        out_specs=(hbm,) * 4,
        scratch_shapes=[
            pltpu.VMEM((TOK, D), bf16),
            pltpu.VMEM((TOK, D), bf16),
            pltpu.VMEM((1, 1), jnp.int32),
            pltpu.VMEM((ACTIONS, D), bf16),
            pltpu.VMEM((1, D), f32),
            pltpu.VMEM((2, TOK), jnp.int32),
            pltpu.VMEM((2, TOK), f32),
            pltpu.VMEM((1, TOK), jnp.int32),
            pltpu.VMEM((TOK, D), bf16),
            pltpu.VMEM((TOK, D), bf16),
            pltpu.VMEM((D // PEERS, FF), bf16),
            pltpu.VMEM((FF // PEERS, D), bf16),
            pltpu.VMEM((D, FF), bf16),
            pltpu.VMEM((FF, D), bf16),
            pltpu.VMEM((PHASES, CHIPS, TOK, HD), bf16),
            pltpu.VMEM((PHASES, CHIPS, 2, TOK, HD), bf16),
            pltpu.VMEM((PHASES, CHIPS, 2, TOK, HD), bf16),
            pltpu.VMEM((PHASES, CHIPS, TOK, HD), bf16),
            pltpu.VMEM((TOK, D), bf16),
            pltpu.VMEM((TOK, D), bf16),
            pltpu.VMEM((2 * TOK, D), bf16),
            pltpu.VMEM((256, 256), bf16),
            pltpu.VMEM((4, 256, 256), bf16),
            pltpu.VMEM((2, TOK, 256), bf16),
            pltpu.VMEM((2, 4, TOK, 256), bf16),
        ]
        + [block] * 2
        + [
            pltpu.VMEM((256, HALF_BLOCK), bf16),
            pltpu.VMEM((256, HALF_BLOCK), bf16),
            pltpu.VMEM((256, HALF_BLOCK + TOK), bf16),
            pltpu.VMEM((256, HALF_BLOCK + TOK), bf16),
            pltpu.VMEM((TOK, 1), f32),
            pltpu.VMEM((ROWS, 1), f32),
            pltpu.VMEM((ROWS, FF), f32),
        ]
        + [block] * 4
        + [
            pltpu.VMEM((PADDED, D), bf16),
            pltpu.VMEM((PADDED, D), bf16),
            pltpu.VMEM((CHIPS, 2, 128, PADDED), bf16),
            pltpu.VMEM((PADDED, FF), bf16),
            pltpu.VMEM((CHIPS, 2, 64, PADDED), bf16),
            pltpu.VMEM((ROWS, FF), f32),
            pltpu.VMEM((PADDED, FF), bf16),
            pltpu.VMEM((PADDED, FF), bf16),
            pltpu.VMEM((TOK, D), f32),
            pltpu.VMEM((CHIPS, 2, 64, D), bf16),
            pltpu.VMEM((CHIPS, 2, 128, FF), bf16),
            pltpu.VMEM((CHIPS, 64, D), bf16),
            pltpu.VMEM((CHIPS, 128, FF), bf16),
            pltpu.VMEM((CHIPS - 1, 32, D), bf16),
            pltpu.VMEM((CHIPS - 1, 32, D), bf16),
            pltpu.VMEM((CHIPS - 1, 64, FF), bf16),
            pltpu.VMEM((CHIPS - 1, 64, FF), bf16),
            dma((8,)),
            dma((4,)),
            dma((2,)),
            dma((5,)),
            dma((PHASES, 3)),
            dma((PHASES, 3, CHIPS)),
            dma((PHASES, 3, CHIPS)),
            dma((PHASES, 2)),
            dma((PHASES, 2)),
            dma((PHASES,)),
            dma((PHASES, CHIPS)),
            dma((PHASES, CHIPS)),
            dma((5, PEERS)),
            dma((5, PEERS)),
            dma((2, CHIPS)),
            dma((2, CHIPS)),
            dma((4, CHIPS - 1)),
            dma((4, CHIPS - 1)),
        ],
        compiler_params=pltpu.CompilerParams(
            collective_id=0, has_side_effects=True, vmem_limit_bytes=62 * 2**20
        ),
        name="layer",
    )(
        tokens.reshape(TOK, D),
        cotangent.reshape(TOK, D),
        actions,
        action_table,
        norm_gain.reshape(1, D),
        routes.reshape(TOK, 2).T,
        gate_probs.reshape(TOK, 2).T,
        predicted.reshape(1, TOK),
        queries.reshape(TOK, D),
        key_rows.reshape(TOK, D),
        values.reshape(TOK, D),
        up_weight.reshape(D, FF),
        down_weight.reshape(FF, D),
    )
    layer_out, stream_grad, up_grad, down_grad = pl.pallas_call(
        deliver_kernel,
        out_shape=results,
        in_specs=[hbm] * 4,
        out_specs=(hbm,) * 4,
        scratch_shapes=[pltpu.VMEM(r.shape, r.dtype) for r in results] + [dma((4,)), dma((4,))],
        name="deliver",
    )(*made)
    return (
        layer_out.reshape(tokens.shape),
        stream_grad.reshape(tokens.shape),
        up_grad.reshape(1, D // PEERS, FF),
        down_grad.reshape(1, FF // PEERS, D),
    )


def solution(mesh):
    rows = P("expert", "tm", None, None)
    in_specs = (
        rows,
        rows,
        rows,
        rows,
        P("expert", "tm"),
        P(),
        P(),
        rows,
        rows,
        P("expert", "tm", None),
        rows,
        P("expert", None, None),
        P("expert", None, None),
    )
    out_specs = (rows, rows, P("expert", "tm", None), P("expert", "tm", None))
    return jax.shard_map(local, mesh=mesh, in_specs=in_specs, out_specs=out_specs, check_vma=False)
```
